512 devices in a mesh: pair: 16 (over z_hi, x, core), aux: 32 (over z_lo, y).
Axes of the slice: x: 4, y: 4, z: 16 (z_hi: 2, z_lo: 8; z = z_hi * 8 + z_lo), core: 2. Of those that a mesh axis runs over, the one named last changes fastest.
Arguments:
- amplitudes: bfloat16 [16, 2048, 2048], P('pair', None, 'aux'), may hold values from -0.125 to 0.125
- fitting: bfloat16 [6144, 4, 2048], P('aux', None, 'pair'), may hold values from -6 to 6
- coefficients: bfloat16 [2048, 2048], P('pair'), may hold values from -0.125 to 0.125
- pair_list: int32 [16, 2], P('pair'), may hold values from 0 to 3, as said below
Outputs:
- density_ao: bfloat16 [6144, 4, 2048], P('aux', None, 'pair')
The draws below stay inside these ranges and needn't reach their ends.
Inputs may be any that keep to these rules, and one draw needn't show every extreme that they name: `pair_list`: column 0 names every internal of the window in exactly 4 rows; column 1 names any internal of the window.
All inputs are finite; a program needn't handle non-finite values.
Results may differ from the reference program's by a relative error of at most 0.015.
Values may be sent and summed in bfloat16 or wider, within the bound.
No kernel may reach another device: no remote copies, remote signals or barrier semaphores. Data moves between devices by JAX's collectives and lax.ppermute only.
A program may use at most 64 MiB of HBM per device.

```python
import jax
import jax.numpy as jnp

V = 2048
NAO = 2048
OCCW = 4
PAIR_DEV = 1
PAIRS = 16
NAUX = 6144
N_PAIR = 16


def draw_pair_list(key, part):
    key = jax.random.fold_in(key, 7)
    first_key, second_key = jax.random.split(key)
    first_index = jax.random.permutation(first_key, PAIRS) % OCCW
    second_index = jax.random.randint(second_key, (PAIRS,), 0, OCCW)
    return jnp.stack([first_index, second_index], axis=1).astype(jnp.int32)


def level_of(stream_key, dims, pieces, low, high):
    def one(position, parts):
        draws = jax.random.uniform(jax.random.fold_in(jax.random.fold_in(stream_key, 6), position), (parts,), jnp.float32, low / len(pieces), high / len(pieces))
        return jnp.repeat(jnp.exp(draws), dims[position] // parts).reshape((-1,) + (1,) * (len(dims) - position - 1))

    gain = one(*pieces[0])
    for cut in pieces[1:]:
        gain = gain * one(*cut)
    return gain


def scatter_about(rng, extent, deviation, reach, pieces=(), dtype=jnp.bfloat16):
    array = jax.random.normal(rng, extent, jnp.float32) * deviation
    if len(pieces) > 0:
        array = level_of(rng, extent, pieces, -0.22, 0.18) * array
    return jnp.clip(array, min=-reach, max=reach).astype(dtype)


def setup_inputs(seed: int = 0) -> dict:
    arg_keys = jax.random.split(jax.random.key(seed), 5)
    amplitudes = scatter_about(arg_keys[0], (PAIRS, V, V), V ** -0.5, 0.125, ((0, 16), (2, 32)))
    fitting = scatter_about(arg_keys[1], (NAUX, OCCW, V), 1.0, 6.0, ((0, 32), (2, 16)))
    coefficients = scatter_about(arg_keys[2], (NAO, V), V ** -0.5, 0.125, ((0, 16),))
    pair_list = draw_pair_list(jax.random.fold_in(arg_keys[4], 71), 0)
    return {"amplitudes": amplitudes, "fitting": fitting, "coefficients": coefficients, "pair_list": pair_list}


def reference(amplitudes, fitting, coefficients, pair_list):
    total = jnp.zeros((NAUX, OCCW, V), jnp.float32)
    for group in range(N_PAIR):
        block_sum = jnp.zeros((NAUX, OCCW, V), jnp.float32)
        for member in range(PAIR_DEV):
            index = group * PAIR_DEV + member
            first_index = pair_list[index, 0]
            second_index = pair_list[index, 1]
            selected = jnp.take(fitting, second_index, axis=1)
            contrib = jnp.dot(selected, amplitudes[index].T, preferred_element_type=jnp.float32)
            block_sum = block_sum.at[:, first_index, :].add(contrib)
        total = total + block_sum.astype(jnp.bfloat16).astype(jnp.float32)
    density_mo = total.astype(jnp.bfloat16)
    flat = density_mo.reshape(NAUX * OCCW, V)
    result = jnp.dot(flat, coefficients.T, preferred_element_type=jnp.float32)
    return result.reshape(NAUX, OCCW, NAO).astype(jnp.bfloat16)
```

```python
import jax
import jax.numpy as jnp
from jax import lax
from jax.experimental import pallas as pl
from jax.experimental.pallas import tpu as pltpu
from jax.sharding import Mesh, PartitionSpec as P

H, X, C, L, Y = 2, 4, 2, 8, 4
AXES = ("h", "x", "c", "l", "y")
OCC = 4


def flat(h, x, c, l, y):
    return (((h * X + x) * C + c) * L + l) * Y + y


def coords():
    for h in range(H):
        for x in range(X):
            for c in range(C):
                for l in range(L):
                    for y in range(Y):
                        yield h, x, c, l, y


def weight_perm(k):
    return [
        (flat(h, x, c, l, y), flat(l // X, l % X, c, (h ^ k) * X + x, y))
        for h, x, c, l, y in coords()
    ]


def result_perm(k):
    return [
        (flat(h, x, c, l, y), flat(l // X, l % X, c, 2 * x + (h ^ k), y))
        for h, x, c, l, y in coords()
    ]


def shift(n, k):
    return [(i, (i + k) % n) for i in range(n)]


def contract_kernel(first_ref, second_ref, w_ref, b_ref, out_ref, acc_ref, s_ref):
    slots, rows, cols = w_ref.shape[1], w_ref.shape[2], w_ref.shape[3]

    @pl.when(pl.program_id(0) == 0)
    def _():
        acc_ref[...] = jnp.zeros_like(acc_ref)

        def add(slot, _):
            first, second = first_ref[slot], second_ref[slot]
            at_col = pl.multiple_of(first * cols, cols)
            for z in range(Y):
                half, part = z // 2, z % 2
                at_row = pl.multiple_of((half * OCC + second) * (2 * rows) + part * rows, rows)
                here = (pl.ds(at_row, rows), pl.ds(at_col, cols))
                acc_ref[here] += w_ref[z, slot].astype(jnp.float32)
            return 0

        lax.fori_loop(0, slots, add, 0)
        s_ref[...] = acc_ref[...].astype(jnp.bfloat16)

    depth = b_ref.shape[2]
    total = jnp.dot(b_ref[0], s_ref[:depth], preferred_element_type=jnp.float32)
    total += jnp.dot(b_ref[1], s_ref[depth:], preferred_element_type=jnp.float32)
    out_ref[...] = total.astype(jnp.bfloat16)


def contract(first, second, w, b, steps=4):
    _, q, depth = b.shape
    cols = w.shape[3]
    block = q // steps
    return pl.pallas_call(
        contract_kernel,
        grid_spec=pltpu.PrefetchScalarGridSpec(
            num_scalar_prefetch=2,
            grid=(steps,),
            in_specs=[
                pl.BlockSpec(w.shape, lambda s, *_: (0, 0, 0, 0)),
                pl.BlockSpec((2, block, depth), lambda s, *_: (0, s, 0)),
            ],
            out_specs=pl.BlockSpec((block, OCC * cols), lambda s, *_: (s, 0)),
            scratch_shapes=[
                pltpu.VMEM((2 * depth, OCC * cols), jnp.float32),
                pltpu.VMEM((2 * depth, OCC * cols), jnp.bfloat16),
            ],
        ),
        out_shape=jax.ShapeDtypeStruct((q, OCC * cols), jnp.bfloat16),
        compiler_params=pltpu.CompilerParams(vmem_limit_bytes=32 * 1024 * 1024),
        cost_estimate=pl.CostEstimate(
            flops=2 * q * 2 * depth * OCC * cols, bytes_accessed=6 * 2**20, transcendentals=0
        ),
    )(first, second, w, b)


def on_device(amplitudes, fitting, coefficients, pair_list):
    x, l, y = lax.axis_index("x"), lax.axis_index("l"), lax.axis_index("y")
    f32, bf16 = jnp.float32, jnp.bfloat16

    q_own, occ, b_own = fitting.shape
    b_all = lax.all_gather(fitting.reshape(q_own, occ * b_own), "l", axis=0, tiled=True)
    b_all = lax.all_gather(b_all, "c", axis=0)
    pairs = lax.all_gather(pair_list, ("h", "x", "c"), axis=0, tiled=True)

    t_own = amplitudes[0].T
    t_all = jnp.concatenate(
        [t_own] + [lax.ppermute(t_own, "x", shift(X, k)) for k in range(1, X)], axis=0
    )

    n_mu = coefficients.shape[0]
    c_near = lax.all_gather(coefficients, "c", axis=0, tiled=True)
    part = n_mu // Y
    piece = lax.dynamic_slice_in_dim(coefficients, y * part, part, 0)
    c_far = lax.all_gather(
        lax.ppermute(piece, "h", shift(H, 1)), ("c", "y"), axis=0, tiled=True
    )

    received = []
    for k, c_part in ((0, c_near), (1, c_far)):
        w = jnp.einsum(
            "na,cma->cnm", t_all, c_part.reshape(C, n_mu, -1), preferred_element_type=f32
        ).astype(bf16)
        received.append(lax.ppermute(w, AXES, weight_perm(k)))
    w = jnp.concatenate(received, axis=1)
    w = lax.all_to_all(w, "c", split_axis=0, concat_axis=0, tiled=True)
    pieces = [w] + [lax.ppermute(w, "y", shift(Y, k)) for k in range(1, Y)]
    w_all = jnp.zeros((Y,) + w.shape, bf16)
    for k, piece in enumerate(pieces):
        w_all = lax.dynamic_update_slice_in_dim(w_all, piece[None], (y - k) % Y, 0)
    rows = t_own.shape[0]
    w_all = w_all.reshape(Y, C * H * X, rows, n_mu)

    slot = jnp.arange(C * H * X, dtype=jnp.int32)
    slot_c, slot_k, slot_x = slot // (H * X), (slot // X) % H, slot % X
    slot_pair = (((l // X) ^ slot_k) * X + (l % X - slot_x) % X) * C + slot_c
    slot_info = jnp.take(pairs, slot_pair, axis=0)

    partial = contract(slot_info[:, 0], slot_info[:, 1], w_all, b_all)

    h = lax.axis_index("h")
    cols = partial.shape[1]
    partial = partial.reshape(X, 2 * q_own, cols)
    partial = lax.all_to_all(partial, "x", split_axis=0, concat_axis=0, tiled=True)
    summed = jnp.sum(partial.astype(f32), axis=0).astype(bf16)
    total = jnp.zeros((q_own, cols), f32)
    for k in range(H):
        piece = lax.dynamic_slice_in_dim(summed, (h ^ k) * q_own, q_own, 0)
        total += lax.ppermute(piece, AXES, result_perm(k)).astype(f32)
    return total.astype(bf16).reshape(q_own, occ, n_mu)


def solution(mesh):
    fine = Mesh(mesh.devices.reshape(H, X, C, L, Y), AXES)
    pair, aux = ("h", "x", "c"), ("l", "y")
    in_specs = (P(pair, None, aux), P(aux, None, pair), P(pair, None), P(pair, None))
    out_specs = P(aux, None, pair)
    return jax.shard_map(
        on_device, mesh=fine, in_specs=in_specs, out_specs=out_specs, check_vma=False
    )
```

```python
import jax
import jax.numpy as jnp
from jax import lax
from jax.experimental import pallas as pl
from jax.experimental.pallas import tpu as pltpu
from jax.sharding import Mesh, PartitionSpec as P

H, X, C, L, Y = 2, 4, 2, 8, 4
AXES = ("h", "x", "c", "l", "y")
OCC = 4


def flat(h, x, c, l, y):
    return (((h * X + x) * C + c) * L + l) * Y + y


def coords():
    for h in range(H):
        for x in range(X):
            for c in range(C):
                for l in range(L):
                    for y in range(Y):
                        yield h, x, c, l, y


def weight_perm(k):
    return [
        (flat(h, x, c, l, y), flat(l // X, l % X, c, (h ^ k) * X + x, y))
        for h, x, c, l, y in coords()
    ]


def result_perm(k):
    return [
        (flat(h, x, c, l, y), flat(l // X, l % X, c, 2 * x + (h ^ k), y))
        for h, x, c, l, y in coords()
    ]


def shift(n, k):
    return [(i, (i + k) % n) for i in range(n)]


def contract_kernel(first_ref, second_ref, where_ref, w_ref, near_ref, far_ref, out_ref, acc_ref, s_ref):
    slots, rows, cols = w_ref.shape[1], w_ref.shape[2], w_ref.shape[3]

    @pl.when(pl.program_id(0) == 0)
    def _():
        acc_ref[...] = jnp.zeros_like(acc_ref)

        def add(slot, _):
            first, second = first_ref[slot], second_ref[slot]
            at_col = pl.multiple_of(first * cols, cols)
            for z in range(Y):
                half, part = z // 2, z % 2
                at_row = pl.multiple_of((half * OCC + second) * (2 * rows) + part * rows, rows)
                here = (pl.ds(at_row, rows), pl.ds(at_col, cols))
                acc_ref[here] += w_ref[z, slot].astype(jnp.float32)
            return 0

        lax.fori_loop(0, slots, add, 0)
        s_ref[...] = acc_ref[...].astype(jnp.bfloat16)

    depth = near_ref.shape[1]
    at_near = pl.multiple_of(where_ref[1] * depth, depth)
    at_far = pl.multiple_of((1 - where_ref[1]) * depth, depth)
    f32 = jnp.float32
    total = jnp.dot(near_ref[...], s_ref[pl.ds(at_near, depth)], preferred_element_type=f32)
    total += jnp.dot(far_ref[...], s_ref[pl.ds(at_far, depth)], preferred_element_type=f32)
    out_ref[...] = total.astype(jnp.bfloat16)


def contract(first, second, where, w, near, far):
    q, depth = near.shape
    cols = w.shape[3]
    block = q // X

    def of_step(s, first, second, where):
        return (where[0] + s + 1) % X, 0

    return pl.pallas_call(
        contract_kernel,
        grid_spec=pltpu.PrefetchScalarGridSpec(
            num_scalar_prefetch=3,
            grid=(X,),
            in_specs=[
                pl.BlockSpec(w.shape, lambda s, *_: (0, 0, 0, 0)),
                pl.BlockSpec((block, depth), of_step),
                pl.BlockSpec((block, depth), of_step),
            ],
            out_specs=pl.BlockSpec((block, OCC * cols), lambda s, *_: (s, 0)),
            scratch_shapes=[
                pltpu.VMEM((2 * depth, OCC * cols), jnp.float32),
                pltpu.VMEM((2 * depth, OCC * cols), jnp.bfloat16),
            ],
        ),
        out_shape=jax.ShapeDtypeStruct((q, OCC * cols), jnp.bfloat16),
        compiler_params=pltpu.CompilerParams(vmem_limit_bytes=32 * 1024 * 1024),
        cost_estimate=pl.CostEstimate(
            flops=2 * q * 2 * depth * OCC * cols, bytes_accessed=6 * 2**20, transcendentals=0
        ),
    )(first, second, where, w, near, far)


def on_device(amplitudes, fitting, coefficients, pair_list):
    h, x, c = lax.axis_index("h"), lax.axis_index("x"), lax.axis_index("c")
    l, y = lax.axis_index("l"), lax.axis_index("y")
    f32, bf16 = jnp.float32, jnp.bfloat16

    def swap_core(v):
        return lax.ppermute(v, "c", shift(C, 1))

    q_own, occ, b_own = fitting.shape
    b_near = lax.all_gather(fitting.reshape(q_own, occ * b_own), "l", axis=0, tiled=True)

    n_mu, n_a = coefficients.shape
    part = n_mu // Y
    piece = lax.dynamic_slice_in_dim(coefficients, y * part, part, 0)
    piece = lax.ppermute(piece, "h", shift(H, 1))
    piece = jnp.broadcast_to(piece[None], (Y, part, n_a))
    c_far = lax.all_to_all(piece, "y", split_axis=0, concat_axis=0, tiled=True)
    c_far = c_far.reshape(n_mu, n_a)

    rows = amplitudes.shape[2]
    info = jnp.pad(pair_list.astype(bf16), ((0, rows - 1), (0, 126)))
    t_own = jnp.concatenate([amplitudes[0].T, info], axis=1)
    t_all = jnp.concatenate(
        [t_own] + [lax.ppermute(t_own, "x", shift(X, k)) for k in range(1, X)], axis=0
    )
    info = t_all.reshape(X, rows, -1)[:, 0, n_a:]
    info = jnp.broadcast_to(jnp.pad(info, ((0, 16 - X), (0, 0)))[None], (C, 16, n_mu))
    t_all = t_all[:, :n_a]

    received = []
    for k, c_part in ((0, coefficients), (1, c_far)):
        w = [
            lax.dot_general(t_all, m, (((1,), (1,)), ((), ())), preferred_element_type=f32)
            for m in (c_part, swap_core(c_part))
        ]
        w = jnp.concatenate([jnp.stack(w).astype(bf16), info], axis=1)
        received.append(lax.ppermute(w, AXES, weight_perm(k)))
    mine = jnp.stack([r[0] for r in received])
    w = jnp.stack([mine, swap_core(jnp.stack([r[1] for r in received]))])
    slots = C * H * X
    n_b = X * rows
    info = w[:, :, n_b : n_b + X, :2].reshape(slots, 2).astype(jnp.int32)
    w = w[:, :, :n_b].reshape(slots, rows, n_mu)
    w, b_near = lax.optimization_barrier((w, b_near))
    pieces = [w] + [lax.ppermute(w, "y", shift(Y, k)) for k in range(1, Y)]
    w_all = jnp.zeros((Y,) + w.shape, bf16)
    for k, piece in enumerate(pieces):
        w_all = lax.dynamic_update_slice_in_dim(w_all, piece[None], (y - k) % Y, 0)
    b_far = swap_core(b_near)

    where = jnp.stack([x, c]).astype(jnp.int32)
    partial = contract(info[:, 0], info[:, 1], where, w_all, b_near, b_far)
    cols = partial.shape[1]
    partial = partial.reshape(X, 2 * q_own, cols)
    summed = partial[X - 1].astype(f32)
    for k in range(1, X):
        summed += lax.ppermute(partial[k - 1], "x", shift(X, k)).astype(f32)
    summed = summed.astype(bf16)

    total = jnp.zeros((q_own, cols), f32)
    for k in range(H):
        piece = lax.dynamic_slice_in_dim(summed, (h ^ k) * q_own, q_own, 0)
        total += lax.ppermute(piece, AXES, result_perm(k)).astype(f32)
    return total.astype(bf16).reshape(q_own, occ, n_mu)


def solution(mesh):
    fine = Mesh(mesh.devices.reshape(H, X, C, L, Y), AXES)
    pair, aux = ("h", "x", "c"), ("l", "y")
    in_specs = (P(pair, None, aux), P(aux, None, pair), P(pair, None), P(pair, None))
    out_specs = P(aux, None, pair)
    return jax.shard_map(
        on_device, mesh=fine, in_specs=in_specs, out_specs=out_specs, check_vma=False
    )
```

```python
import jax
import jax.numpy as jnp
from jax import lax
from jax.experimental import pallas as pl
from jax.experimental.pallas import tpu as pltpu
from jax.sharding import Mesh, PartitionSpec as P

H, X, C, L, Y = 2, 4, 2, 8, 4
AXES = ("h", "x", "c", "l", "y")
OCC = 4


def flat(h, x, c, l, y):
    return (((h * X + x) * C + c) * L + l) * Y + y


def coords():
    for h in range(H):
        for x in range(X):
            for c in range(C):
                for l in range(L):
                    for y in range(Y):
                        yield h, x, c, l, y


def weight_perm(k):
    return [
        (flat(h, x, c, l, y), flat(l // X, l % X, c, (h ^ k) * X + x, y))
        for h, x, c, l, y in coords()
    ]


def result_perm(k):
    return [
        (flat(h, x, c, l, y), flat(l // X, l % X, c, 2 * x + (h ^ k), y))
        for h, x, c, l, y in coords()
    ]


def shift(n, k):
    return [(i, (i + k) % n) for i in range(n)]


def assemble(first_ref, second_ref, w_refs, acc_ref, s_ref):
    acc_ref[...] = jnp.zeros_like(acc_ref)
    offset = 0
    for w_ref in w_refs:
        slots, rows, cols = w_ref.shape[1:]

        def add(slot, _, w_ref=w_ref, offset=offset):
            first, second = first_ref[slot + offset], second_ref[slot + offset]
            at_col = pl.multiple_of(first * cols, cols)
            for z in range(Y):
                half, part = z // 2, z % 2
                at_row = pl.multiple_of((half * OCC + second) * (2 * rows) + part * rows, rows)
                here = (pl.ds(at_row, rows), pl.ds(at_col, cols))
                acc_ref[here] += w_ref[z, slot].astype(jnp.float32)
            return 0

        lax.fori_loop(0, slots, add, 0)
        offset += slots
    s_ref[...] = acc_ref[...].astype(jnp.bfloat16)


def multiply(where_ref, near_ref, far_ref, s_ref, out_ref):
    depth = near_ref.shape[1]
    at_near = pl.multiple_of(where_ref[1] * depth, depth)
    at_far = pl.multiple_of((1 - where_ref[1]) * depth, depth)
    f32 = jnp.float32
    total = jnp.dot(near_ref[...], s_ref[pl.ds(at_near, depth)], preferred_element_type=f32)
    total += jnp.dot(far_ref[...], s_ref[pl.ds(at_far, depth)], preferred_element_type=f32)
    out_ref[...] = total.astype(jnp.bfloat16)


def first_kernel(
    first_ref, second_ref, where_ref, w0_ref, w1_ref, near_ref, far_ref, out_ref, s_ref, acc_ref
):
    @pl.when(pl.program_id(0) == 0)
    def _():
        assemble(first_ref, second_ref, (w0_ref, w1_ref), acc_ref, s_ref)

    multiply(where_ref, near_ref, far_ref, s_ref, out_ref)


def second_kernel(where_ref, near_ref, far_ref, s_ref, out_ref):
    multiply(where_ref, near_ref, far_ref, s_ref, out_ref)


def part_of(k):
    return lambda s, *refs: (2 * s + (refs[-1][0] ^ k), 0)


def whole(array):
    return pl.BlockSpec(array.shape, lambda s, *_: (0,) * array.ndim)


def contract(first, second, where, w0, w1, near, far):
    q, depth = near.shape
    cols = OCC * w0.shape[3]
    block = q // (2 * X)
    out = jax.ShapeDtypeStruct((q // 2, cols), jnp.bfloat16)
    out_spec = pl.BlockSpec((block, cols), lambda s, *_: (s, 0))
    s_shape = jax.ShapeDtypeStruct((2 * depth, cols), jnp.bfloat16)
    params = pltpu.CompilerParams(vmem_limit_bytes=32 * 1024 * 1024)
    cost = pl.CostEstimate(
        flops=2 * q * depth * cols, bytes_accessed=4 * 2**20, transcendentals=0
    )
    rows = [pl.BlockSpec((block, depth), part_of(0))] * 2
    one, s = pl.pallas_call(
        first_kernel,
        grid_spec=pltpu.PrefetchScalarGridSpec(
            num_scalar_prefetch=3,
            grid=(X,),
            in_specs=[whole(w0), whole(w1)] + rows,
            out_specs=[out_spec, whole(s_shape)],
            scratch_shapes=[pltpu.VMEM(s_shape.shape, jnp.float32)],
        ),
        out_shape=[out, s_shape],
        compiler_params=params,
        cost_estimate=cost,
    )(first, second, where, w0, w1, near, far)
    rows = [pl.BlockSpec((block, depth), part_of(1))] * 2
    two = pl.pallas_call(
        second_kernel,
        grid_spec=pltpu.PrefetchScalarGridSpec(
            num_scalar_prefetch=1, grid=(X,), in_specs=rows + [whole(s)], out_specs=out_spec
        ),
        out_shape=out,
        compiler_params=params,
        cost_estimate=cost,
    )(where, near, far, s)
    return one, two


def on_device(amplitudes, fitting, coefficients, pair_list):
    h, x, c = lax.axis_index("h"), lax.axis_index("x"), lax.axis_index("c")
    y = lax.axis_index("y")
    f32, bf16 = jnp.float32, jnp.bfloat16

    def swap_core(v):
        return lax.ppermute(v, "c", shift(C, 1))

    def gather_y(v):
        v = jnp.broadcast_to(v[None], (Y,) + v.shape)
        return lax.all_to_all(v, "y", split_axis=0, concat_axis=0, tiled=True)

    q_own, occ, b_own = fitting.shape
    b_near = lax.all_gather(fitting.reshape(q_own, occ * b_own), "l", axis=0, tiled=True)

    n_mu, n_a = coefficients.shape
    part = n_mu // Y
    mirror = [(i, H * L - 1 - i) for i in range(H * L)]
    piece = lax.dynamic_slice_in_dim(coefficients, y * part, part, 0)
    piece = lax.ppermute(piece, ("h", "l"), mirror)

    rows = amplitudes.shape[2]
    info = jnp.pad(pair_list.astype(bf16), ((0, rows - 1), (0, 126)))
    t_own = jnp.concatenate([amplitudes[0].T, info], axis=1)
    t_all = jnp.concatenate(
        [t_own] + [lax.ppermute(t_own, "x", shift(X, k)) for k in range(1, X)], axis=0
    )
    info = t_all.reshape(X, rows, -1)[:, 0, n_a:]
    info = jnp.broadcast_to(jnp.pad(info, ((0, 16 - X), (0, 0)))[None], (C, 16, n_mu))
    t_all = t_all[:, :n_a]

    slots, n_b = C * X, X * rows
    w_all, w_info = [], []
    for k in range(H):
        c_part = gather_y(piece).reshape(n_mu, n_a) if k else coefficients
        w = [
            lax.dot_general(t_all, m, (((1,), (1,)), ((), ())), preferred_element_type=f32)
            for m in (c_part, swap_core(c_part))
        ]
        w = jnp.concatenate([jnp.stack(w).astype(bf16), info], axis=1)
        if k == 0:
            w, piece = lax.optimization_barrier((w, piece))
        w = lax.ppermute(w, AXES, weight_perm(k))
        w = jnp.stack([w[0], swap_core(w[1])])
        w_info.append(w[:, n_b : n_b + X, :2].reshape(slots, 2).astype(jnp.int32))
        w = w[:, :n_b].reshape(slots, rows, n_mu)
        if k:
            w, b_near = lax.optimization_barrier((w, b_near))
        w_all.append(gather_y(w).reshape(Y, slots, rows, n_mu))
    info = jnp.concatenate(w_info)
    b_far = swap_core(b_near)

    where = jnp.stack([h, c]).astype(jnp.int32)
    parts = contract(info[:, 0], info[:, 1], where, w_all[0], w_all[1], b_near, b_far)
    total = 0
    for k, v in enumerate(parts):
        v = v.reshape(X, q_own, -1)
        v = lax.all_to_all(v, "x", split_axis=0, concat_axis=0, tiled=True)
        v = jnp.sum(v.astype(f32), axis=0).astype(bf16)
        total += lax.ppermute(v, AXES, result_perm(k)).astype(f32)
    return total.astype(bf16).reshape(q_own, occ, n_mu)


def solution(mesh):
    fine = Mesh(mesh.devices.reshape(H, X, C, L, Y), AXES)
    pair, aux = ("h", "x", "c"), ("l", "y")
    in_specs = (P(pair, None, aux), P(aux, None, pair), P(pair, None), P(pair, None))
    out_specs = P(aux, None, pair)
    return jax.shard_map(
        on_device, mesh=fine, in_specs=in_specs, out_specs=out_specs, check_vma=False
    )
```

```python
import jax
import jax.numpy as jnp
from jax import lax
from jax.experimental import pallas as pl
from jax.experimental.pallas import tpu as pltpu
from jax.sharding import Mesh, PartitionSpec as P

H, X, C, L, Y = 2, 4, 2, 8, 4
AXES = ("h", "x", "c", "l", "y")
OCC = 4


def flat(h, x, c, l, y):
    return (((h * X + x) * C + c) * L + l) * Y + y


def coords():
    for h in range(H):
        for x in range(X):
            for c in range(C):
                for l in range(L):
                    for y in range(Y):
                        yield h, x, c, l, y


INNER, OUTER = (2, 3, 4, 5), (7, 6, 1, 0)


def place(h, h2, x2):
    l = (INNER if h2 == h else OUTER)[x2]
    return l if h == 0 else L - 1 - l


def chunk(h, l):
    return next((h2, x2) for h2 in range(H) for x2 in range(X) if place(h, h2, x2) == l)


def weight_perm(k):
    return [
        (flat(h, x, c, l, y), flat(l // X, l % X, c, place(l // X, h ^ k, x), y))
        for h, x, c, l, y in coords()
    ]


def result_perm(k):
    return [
        (flat(h, x, c, l, y), flat(*chunk(h, l), c, L - 1 - x if h ^ k else x, y))
        for h, x, c, l, y in coords()
    ]


def shift(n, k):
    return [(i, (i + k) % n) for i in range(n)]


def contract_kernel(first_ref, second_ref, where_ref, w_ref, near_ref, far_ref, out_ref, acc_ref, s_ref):
    slots, rows, cols = w_ref.shape[1], w_ref.shape[2], w_ref.shape[3]

    @pl.when(pl.program_id(0) == 0)
    def _():
        acc_ref[...] = jnp.zeros_like(acc_ref)

        def add(slot, _):
            first, second = first_ref[slot], second_ref[slot]
            at_col = pl.multiple_of(first * cols, cols)
            for z in range(Y):
                half, part = z // 2, z % 2
                at_row = pl.multiple_of((half * OCC + second) * (2 * rows) + part * rows, rows)
                here = (pl.ds(at_row, rows), pl.ds(at_col, cols))
                acc_ref[here] += w_ref[z, slot].astype(jnp.float32)
            return 0

        lax.fori_loop(0, slots, add, 0)
        s_ref[...] = acc_ref[...].astype(jnp.bfloat16)

    depth = near_ref.shape[1]
    at_near = pl.multiple_of(where_ref[1] * depth, depth)
    at_far = pl.multiple_of((1 - where_ref[1]) * depth, depth)
    f32 = jnp.float32
    total = jnp.dot(near_ref[...], s_ref[pl.ds(at_near, depth)], preferred_element_type=f32)
    total += jnp.dot(far_ref[...], s_ref[pl.ds(at_far, depth)], preferred_element_type=f32)
    out_ref[...] = total.astype(jnp.bfloat16)


def contract(first, second, where, w, near, far):
    q, depth = near.shape
    cols = w.shape[3]
    block = q // L

    def of_step(s, first, second, where):
        to = (where[0] + s // 2 + 1) % X
        return jnp.where(s % 2 == 0, to, L - 1 - to), 0

    return pl.pallas_call(
        contract_kernel,
        grid_spec=pltpu.PrefetchScalarGridSpec(
            num_scalar_prefetch=3,
            grid=(L,),
            in_specs=[
                pl.BlockSpec(w.shape, lambda s, *_: (0, 0, 0, 0)),
                pl.BlockSpec((block, depth), of_step),
                pl.BlockSpec((block, depth), of_step),
            ],
            out_specs=pl.BlockSpec((block, OCC * cols), lambda s, *_: (s, 0)),
            scratch_shapes=[
                pltpu.VMEM((2 * depth, OCC * cols), jnp.float32),
                pltpu.VMEM((2 * depth, OCC * cols), jnp.bfloat16),
            ],
        ),
        out_shape=jax.ShapeDtypeStruct((q, OCC * cols), jnp.bfloat16),
        compiler_params=pltpu.CompilerParams(vmem_limit_bytes=32 * 1024 * 1024),
        cost_estimate=pl.CostEstimate(
            flops=2 * q * 2 * depth * OCC * cols, bytes_accessed=6 * 2**20, transcendentals=0
        ),
    )(first, second, where, w, near, far)


def on_device(amplitudes, fitting, coefficients, pair_list):
    h, x, c = lax.axis_index("h"), lax.axis_index("x"), lax.axis_index("c")
    l, y = lax.axis_index("l"), lax.axis_index("y")
    f32, bf16 = jnp.float32, jnp.bfloat16

    def swap_core(v):
        return lax.ppermute(v, "c", shift(C, 1))

    n_mu, n_a = coefficients.shape
    part = n_mu // Y
    mirror = [(i, H * L - 1 - i) for i in range(H * L)]
    piece = lax.dynamic_slice_in_dim(coefficients, y * part, part, 0)
    piece = lax.ppermute(piece, ("h", "l"), mirror)

    q_own, occ, b_own = fitting.shape
    rows = amplitudes.shape[2]
    info = jnp.pad(pair_list.astype(bf16), ((0, rows - 1), (0, 126)))
    t_own = jnp.concatenate([amplitudes[0].T, info], axis=1)
    b_near = fitting.reshape(q_own, occ * b_own)
    piece, t_own, b_near = lax.optimization_barrier((piece, t_own, b_near))

    b_near = lax.all_gather(b_near, "l", axis=0, tiled=True)

    t_all = jnp.concatenate(
        [t_own] + [lax.ppermute(t_own, "x", shift(X, k)) for k in range(1, X)], axis=0
    )
    piece = jnp.broadcast_to(piece[None], (Y, part, n_a))
    c_far = lax.all_to_all(piece, "y", split_axis=0, concat_axis=0, tiled=True)
    c_far = c_far.reshape(n_mu, n_a)

    info = t_all.reshape(X, rows, -1)[:, 0, n_a:]
    info = jnp.broadcast_to(jnp.pad(info, ((0, 16 - X), (0, 0)))[None], (C, 16, n_mu))
    t_all = t_all[:, :n_a]

    received = []
    for k, c_part in ((0, coefficients), (1, c_far)):
        w = [
            lax.dot_general(t_all, m, (((1,), (1,)), ((), ())), preferred_element_type=f32)
            for m in (c_part, swap_core(c_part))
        ]
        w = jnp.concatenate([jnp.stack(w).astype(bf16), info], axis=1)
        received.append(lax.ppermute(w, AXES, weight_perm(k)))
    mine = jnp.stack([r[0] for r in received])
    w = jnp.stack([mine, swap_core(jnp.stack([r[1] for r in received]))])
    slots = C * H * X
    n_b = X * rows
    info = w[:, :, n_b : n_b + X, :2].reshape(slots, 2).astype(jnp.int32)
    w = w[:, :, :n_b].reshape(slots, rows, n_mu)
    w, b_near = lax.optimization_barrier((w, b_near))
    pieces = [w] + [lax.ppermute(w, "y", shift(Y, k)) for k in range(1, Y)]
    w_all = jnp.zeros((Y,) + w.shape, bf16)
    for k, piece in enumerate(pieces):
        w_all = lax.dynamic_update_slice_in_dim(w_all, piece[None], (y - k) % Y, 0)
    b_far = swap_core(b_near)

    where = jnp.stack([x, c]).astype(jnp.int32)
    partial = contract(info[:, 0], info[:, 1], where, w_all, b_near, b_far)
    cols = partial.shape[1]
    partial = partial.reshape(X, 2 * q_own, cols)
    summed = partial[X - 1].astype(f32)
    for k in range(1, X):
        summed += lax.ppermute(partial[k - 1], "x", shift(X, k)).astype(f32)
    summed = summed.astype(bf16)

    total = jnp.zeros((q_own, cols), f32)
    for k in range(H):
        piece = lax.dynamic_slice_in_dim(summed, (h ^ k) * q_own, q_own, 0)
        total += lax.ppermute(piece, AXES, result_perm(k)).astype(f32)
    return total.astype(bf16).reshape(q_own, occ, n_mu)


def solution(mesh):
    fine = Mesh(mesh.devices.reshape(H, X, C, L, Y), AXES)
    pair, aux = ("h", "x", "c"), ("l", "y")
    in_specs = (P(pair, None, aux), P(aux, None, pair), P(pair, None), P(pair, None))
    out_specs = P(aux, None, pair)
    return jax.shard_map(
        on_device, mesh=fine, in_specs=in_specs, out_specs=out_specs, check_vma=False
    )
```

```python
import jax
import jax.numpy as jnp
from jax import lax
from jax.experimental import pallas as pl
from jax.experimental.pallas import tpu as pltpu
from jax.sharding import Mesh, PartitionSpec as P

H, X, C, L, Y = 2, 4, 2, 8, 4
AXES = ("h", "x", "c", "l", "y")
OCC = 4


def flat(h, x, c, l, y):
    return (((h * X + x) * C + c) * L + l) * Y + y


def coords():
    for h in range(H):
        for x in range(X):
            for c in range(C):
                for l in range(L):
                    for y in range(Y):
                        yield h, x, c, l, y


INNER, OUTER = (2, 3, 4, 5), (7, 6, 1, 0)


def place(h, h2, x2):
    l = (INNER if h2 == h else OUTER)[x2]
    return l if h == 0 else L - 1 - l


def chunk(h, l):
    return next((h2, x2) for h2 in range(H) for x2 in range(X) if place(h, h2, x2) == l)


def weight_perm(k):
    return [
        (flat(h, x, c, l, y), flat(l // X, l % X, c, place(l // X, h ^ k, x), y))
        for h, x, c, l, y in coords()
    ]


def result_perm(k):
    return [
        (flat(h, x, c, l, y), flat(*chunk(h, l), c, L - 1 - x if h ^ k else x, y))
        for h, x, c, l, y in coords()
    ]


def shift(n, k):
    return [(i, (i + k) % n) for i in range(n)]


def assemble(first_ref, second_ref, w_ref, acc_ref, s_ref):
    slots, rows, cols = w_ref.shape[1:]
    acc_ref[...] = jnp.zeros_like(acc_ref)

    def add(slot, _):
        first, second = first_ref[slot], second_ref[slot]
        at_col = pl.multiple_of(first * cols, cols)
        for z in range(Y):
            half, part = z // 2, z % 2
            at_row = pl.multiple_of((half * OCC + second) * (2 * rows) + part * rows, rows)
            here = (pl.ds(at_row, rows), pl.ds(at_col, cols))
            acc_ref[here] += w_ref[z, slot].astype(jnp.float32)
        return 0

    lax.fori_loop(0, slots, add, 0)
    s_ref[...] = acc_ref[...].astype(jnp.bfloat16)


def multiply(where_ref, near_ref, far_ref, s_ref, out_ref):
    depth = near_ref.shape[1]
    at_near = pl.multiple_of(where_ref[1] * depth, depth)
    at_far = pl.multiple_of((1 - where_ref[1]) * depth, depth)
    f32 = jnp.float32
    total = jnp.dot(near_ref[...], s_ref[pl.ds(at_near, depth)], preferred_element_type=f32)
    total += jnp.dot(far_ref[...], s_ref[pl.ds(at_far, depth)], preferred_element_type=f32)
    out_ref[...] = total.astype(jnp.bfloat16)


def first_kernel(
    first_ref, second_ref, where_ref, w_ref, near_ref, far_ref, out_ref, s_ref, acc_ref
):
    @pl.when(pl.program_id(0) == 0)
    def _():
        assemble(first_ref, second_ref, w_ref, acc_ref, s_ref)

    multiply(where_ref, near_ref, far_ref, s_ref, out_ref)


def second_kernel(where_ref, near_ref, far_ref, s_ref, out_ref):
    multiply(where_ref, near_ref, far_ref, s_ref, out_ref)


def part_of(k):
    def block(s, *refs):
        where_ref = refs[-1]
        to = (where_ref[2] + s + 1) % X
        return jnp.where((where_ref[0] ^ k) == 0, to, L - 1 - to), 0

    return block


def whole(array):
    return pl.BlockSpec(array.shape, lambda s, *_: (0,) * array.ndim)


def contract(first, second, where, w, near, far):
    q, depth = near.shape
    cols = OCC * w.shape[3]
    block = q // (2 * X)
    out = jax.ShapeDtypeStruct((q // 2, cols), jnp.bfloat16)
    out_spec = pl.BlockSpec((block, cols), lambda s, *_: (s, 0))
    s_shape = jax.ShapeDtypeStruct((2 * depth, cols), jnp.bfloat16)
    params = pltpu.CompilerParams(vmem_limit_bytes=32 * 1024 * 1024)
    cost = pl.CostEstimate(
        flops=2 * q * depth * cols, bytes_accessed=4 * 2**20, transcendentals=0
    )
    rows = [pl.BlockSpec((block, depth), part_of(0))] * 2
    one, s = pl.pallas_call(
        first_kernel,
        grid_spec=pltpu.PrefetchScalarGridSpec(
            num_scalar_prefetch=3,
            grid=(X,),
            in_specs=[whole(w)] + rows,
            out_specs=[out_spec, whole(s_shape)],
            scratch_shapes=[pltpu.VMEM(s_shape.shape, jnp.float32)],
        ),
        out_shape=[out, s_shape],
        compiler_params=params,
        cost_estimate=cost,
    )(first, second, where, w, near, far)
    rows = [pl.BlockSpec((block, depth), part_of(1))] * 2
    two = pl.pallas_call(
        second_kernel,
        grid_spec=pltpu.PrefetchScalarGridSpec(
            num_scalar_prefetch=1, grid=(X,), in_specs=rows + [whole(s)], out_specs=out_spec
        ),
        out_shape=out,
        compiler_params=params,
        cost_estimate=cost,
    )(where, near, far, s)
    return one, two


def on_device(amplitudes, fitting, coefficients, pair_list):
    h, x, c = lax.axis_index("h"), lax.axis_index("x"), lax.axis_index("c")
    y = lax.axis_index("y")
    f32, bf16 = jnp.float32, jnp.bfloat16

    def swap_core(v):
        return lax.ppermute(v, "c", shift(C, 1))

    q_own, occ, b_own = fitting.shape
    b_near = fitting.reshape(q_own, occ * b_own)
    b_near, coefficients, amplitudes = lax.optimization_barrier(
        (b_near, coefficients, amplitudes)
    )
    b_near = lax.all_gather(b_near, "l", axis=0, tiled=True)

    n_mu, n_a = coefficients.shape
    part = n_mu // Y
    mirror = [(i, H * L - 1 - i) for i in range(H * L)]
    piece = lax.dynamic_slice_in_dim(coefficients, y * part, part, 0)
    piece = lax.ppermute(piece, ("h", "l"), mirror)

    rows = amplitudes.shape[2]
    info = jnp.pad(pair_list.astype(bf16), ((0, rows - 1), (0, 126)))
    t_own = jnp.concatenate([amplitudes[0].T, info], axis=1)
    c_other = swap_core(coefficients)
    c_other, t_own = lax.optimization_barrier((c_other, t_own))

    t_all = jnp.concatenate(
        [t_own] + [lax.ppermute(t_own, "x", shift(X, k)) for k in range(1, X)], axis=0
    )
    info = t_all.reshape(X, rows, -1)[:, 0, n_a:]
    info = jnp.broadcast_to(jnp.pad(info, ((0, 16 - X), (0, 0)))[None], (C, 16, n_mu))
    t_all = t_all[:, :n_a]

    slots, n_b = H * C * X, X * rows

    def weights(*parts):
        w = [
            lax.dot_general(t_all, m, (((1,), (1,)), ((), ())), preferred_element_type=f32)
            for m in parts
        ]
        return jnp.concatenate([jnp.stack(w).astype(bf16), info], axis=1)

    def send(w, k):
        w = lax.ppermute(w, AXES, weight_perm(k))
        return w[0], swap_core(w[1])

    w_near, piece = lax.optimization_barrier((weights(coefficients, c_other), piece))
    w_near = send(w_near, 0)
    piece = jnp.broadcast_to(piece[None], (Y, part, n_a))
    c_far = lax.all_to_all(piece, "y", split_axis=0, concat_axis=0, tiled=True)
    c_far = c_far.reshape(n_mu, n_a)
    w_far = send(weights(c_far, swap_core(c_far)), 1)

    w = jnp.stack(w_near + w_far)
    pairs = w[:, n_b : n_b + X, :2].reshape(slots, 2).astype(jnp.int32)
    w = w[:, :n_b].reshape(slots, rows, n_mu)
    w, b_near = lax.optimization_barrier((w, b_near))
    pieces = [w] + [lax.ppermute(w, "y", shift(Y, k)) for k in range(1, Y)]
    w_all = jnp.zeros((Y,) + w.shape, bf16)
    for k, piece in enumerate(pieces):
        w_all = lax.dynamic_update_slice_in_dim(w_all, piece[None], (y - k) % Y, 0)
    b_far = swap_core(b_near)

    where = jnp.stack([h, c, x]).astype(jnp.int32)
    parts = contract(pairs[:, 0], pairs[:, 1], where, w_all, b_near, b_far)
    total = 0
    for k, v in enumerate(parts):
        v = v.reshape(X, q_own, -1)
        summed = v[X - 1].astype(f32)
        for n in range(1, X):
            summed += lax.ppermute(v[n - 1], "x", shift(X, n)).astype(f32)
        total += lax.ppermute(summed.astype(bf16), AXES, result_perm(k)).astype(f32)
    return total.astype(bf16).reshape(q_own, occ, n_mu)


def solution(mesh):
    fine = Mesh(mesh.devices.reshape(H, X, C, L, Y), AXES)
    pair, aux = ("h", "x", "c"), ("l", "y")
    in_specs = (P(pair, None, aux), P(aux, None, pair), P(pair, None), P(pair, None))
    out_specs = P(aux, None, pair)
    return jax.shard_map(
        on_device, mesh=fine, in_specs=in_specs, out_specs=out_specs, check_vma=False
    )
```

```python
import jax
import jax.numpy as jnp
from jax import lax
from jax.experimental import pallas as pl
from jax.experimental.pallas import tpu as pltpu
from jax.sharding import Mesh, PartitionSpec as P

H, X, C, L, Y = 2, 4, 2, 8, 4
AXES = ("h", "x", "c", "l", "y")
OCC = 4


def flat(h, x, c, l, y):
    return (((h * X + x) * C + c) * L + l) * Y + y


def coords():
    for h in range(H):
        for x in range(X):
            for c in range(C):
                for l in range(L):
                    for y in range(Y):
                        yield h, x, c, l, y


INNER, OUTER = (2, 3, 4, 5), (7, 6, 1, 0)


def place(h, h2, x2):
    l = (INNER if h2 == h else OUTER)[x2]
    return l if h == 0 else L - 1 - l


def chunk(h, l):
    return next((h2, x2) for h2 in range(H) for x2 in range(X) if place(h, h2, x2) == l)


def weight_perm(k, d):
    return [
        (flat(h, x, c, l, y), flat(l // X, l % X, c ^ d, place(l // X, h ^ k, x), y))
        for h, x, c, l, y in coords()
    ]


def result_perm(k):
    return [
        (flat(h, x, c, l, y), flat(*chunk(h, l), c, L - 1 - x if h ^ k else x, y))
        for h, x, c, l, y in coords()
    ]


def shift(n, k):
    return [(i, (i + k) % n) for i in range(n)]


def contract_kernel(first_ref, second_ref, where_ref, w_ref, near_ref, far_ref, out_ref, acc_ref, s_ref):
    slots, rows, cols = w_ref.shape[1], w_ref.shape[2], w_ref.shape[3]

    @pl.when(pl.program_id(0) == 0)
    def _():
        acc_ref[...] = jnp.zeros_like(acc_ref)

        def add(slot, _):
            first, second = first_ref[slot], second_ref[slot]
            at_col = pl.multiple_of(first * cols, cols)
            for z in range(Y):
                half, part = z // 2, z % 2
                at_row = pl.multiple_of((half * OCC + second) * (2 * rows) + part * rows, rows)
                here = (pl.ds(at_row, rows), pl.ds(at_col, cols))
                acc_ref[here] += w_ref[z, slot].astype(jnp.float32)
            return 0

        lax.fori_loop(0, slots, add, 0)
        s_ref[...] = acc_ref[...].astype(jnp.bfloat16)

    depth = near_ref.shape[1]
    at_near = pl.multiple_of(where_ref[1] * depth, depth)
    at_far = pl.multiple_of((1 - where_ref[1]) * depth, depth)
    f32 = jnp.float32
    total = jnp.dot(near_ref[...], s_ref[pl.ds(at_near, depth)], preferred_element_type=f32)
    total += jnp.dot(far_ref[...], s_ref[pl.ds(at_far, depth)], preferred_element_type=f32)
    out_ref[...] = total.astype(jnp.bfloat16)


def contract(first, second, where, w, near, far):
    q, depth = near.shape
    cols = w.shape[3]
    block = q // L

    def of_step(s, first, second, where):
        to = (where[0] + s // 2 + 1) % X
        return jnp.where(s % 2 == 0, to, L - 1 - to), 0

    return pl.pallas_call(
        contract_kernel,
        grid_spec=pltpu.PrefetchScalarGridSpec(
            num_scalar_prefetch=3,
            grid=(L,),
            in_specs=[
                pl.BlockSpec(w.shape, lambda s, *_: (0, 0, 0, 0)),
                pl.BlockSpec((block, depth), of_step),
                pl.BlockSpec((block, depth), of_step),
            ],
            out_specs=pl.BlockSpec((block, OCC * cols), lambda s, *_: (s, 0)),
            scratch_shapes=[
                pltpu.VMEM((2 * depth, OCC * cols), jnp.float32),
                pltpu.VMEM((2 * depth, OCC * cols), jnp.bfloat16),
            ],
        ),
        out_shape=jax.ShapeDtypeStruct((q, OCC * cols), jnp.bfloat16),
        compiler_params=pltpu.CompilerParams(vmem_limit_bytes=32 * 1024 * 1024),
        cost_estimate=pl.CostEstimate(
            flops=2 * q * 2 * depth * OCC * cols, bytes_accessed=6 * 2**20, transcendentals=0
        ),
    )(first, second, where, w, near, far)


def on_device(amplitudes, fitting, coefficients, pair_list):
    h, x, c = lax.axis_index("h"), lax.axis_index("x"), lax.axis_index("c")
    y = lax.axis_index("y")
    f32, bf16 = jnp.float32, jnp.bfloat16

    def swap_core(v):
        return lax.ppermute(v, "c", shift(C, 1))

    def gather(v, axes, n):
        v = jnp.broadcast_to(v[None], (n,) + v.shape)
        return lax.all_to_all(v, axes, split_axis=0, concat_axis=0, tiled=True)

    q_own, occ, b_own = fitting.shape
    b_near = lax.all_gather(fitting, "l", axis=0, tiled=True)

    n_mu, n_a = coefficients.shape
    part = n_mu // Y
    c_other = swap_core(coefficients)
    mirror = [(i, H * L - 1 - i) for i in range(H * L)]
    piece = lax.dynamic_slice_in_dim(coefficients, y * part, part, 0)
    piece = lax.ppermute(piece, ("h", "l"), mirror)

    rows = amplitudes.shape[2]
    info = jnp.pad(pair_list.astype(bf16), ((0, rows - 1), (0, 126)))
    t_own = jnp.concatenate([amplitudes[0].T, info], axis=1)
    c_other, t_own = lax.optimization_barrier((c_other, t_own))
    t_all = gather(t_own, "x", X)
    t_all, piece = lax.optimization_barrier((t_all, piece))
    info = t_all[:, 0, n_a:]
    info = jnp.pad(info, ((0, 16 - X), (0, 0)))
    t_all = t_all.reshape(X * rows, -1)[:, :n_a]
    c_far = gather(piece, ("c", "y"), C * Y).reshape(C * n_mu, n_a)

    def weights(m):
        return lax.dot_general(
            t_all, m, (((1,), (1,)), ((), ())), preferred_element_type=f32
        ).astype(bf16)

    near = [weights(coefficients), weights(c_other)]
    far = weights(c_far)
    far = [lax.dynamic_slice_in_dim(far, (c ^ d) * n_mu, n_mu, 1) for d in range(C)]
    w = [
        lax.ppermute(jnp.concatenate([v, info], axis=0), AXES, weight_perm(k, d))
        for k, pieces in enumerate((near, far))
        for d, v in enumerate(pieces)
    ]
    w = jnp.stack(w)
    slots, n_b = H * C * X, X * rows
    pairs = w[:, n_b : n_b + X, :2].reshape(slots, 2).astype(jnp.int32)
    w = w[:, :n_b].reshape(slots, rows, n_mu)

    w, b_near = lax.optimization_barrier((w, b_near))
    pieces = [w] + [lax.ppermute(w, "y", shift(Y, k)) for k in range(1, Y)]
    w_all = jnp.zeros((Y,) + w.shape, bf16)
    for k, piece in enumerate(pieces):
        w_all = lax.dynamic_update_slice_in_dim(w_all, piece[None], (y - k) % Y, 0)
    b_near = b_near.reshape(-1, occ * b_own)
    b_far = swap_core(b_near)

    where = jnp.stack([x, c]).astype(jnp.int32)
    partial = contract(pairs[:, 0], pairs[:, 1], where, w_all, b_near, b_far)
    cols = partial.shape[1]
    partial = partial.reshape(X, 2 * q_own, cols)
    summed = partial[X - 1].astype(f32)
    for k in range(1, X):
        summed += lax.ppermute(partial[k - 1], "x", shift(X, k)).astype(f32)
    summed = summed.astype(bf16)

    total = jnp.zeros((q_own, cols), f32)
    for k in range(H):
        piece = lax.dynamic_slice_in_dim(summed, (h ^ k) * q_own, q_own, 0)
        total += lax.ppermute(piece, AXES, result_perm(k)).astype(f32)
    return total.astype(bf16).reshape(q_own, occ, n_mu)


def solution(mesh):
    fine = Mesh(mesh.devices.reshape(H, X, C, L, Y), AXES)
    pair, aux = ("h", "x", "c"), ("l", "y")
    in_specs = (P(pair, None, aux), P(aux, None, pair), P(pair, None), P(pair, None))
    out_specs = P(aux, None, pair)
    return jax.shard_map(
        on_device, mesh=fine, in_specs=in_specs, out_specs=out_specs, check_vma=False
    )
```

```python
import jax
import jax.numpy as jnp
from jax import lax
from jax.experimental import pallas as pl
from jax.experimental.pallas import tpu as pltpu
from jax.sharding import Mesh, PartitionSpec as P

H, X, C, L, Y = 2, 4, 2, 8, 4
AXES = ("h", "x", "c", "l", "y")
OCC = 4


def flat(h, x, c, l, y):
    return (((h * X + x) * C + c) * L + l) * Y + y


def coords():
    for h in range(H):
        for x in range(X):
            for c in range(C):
                for l in range(L):
                    for y in range(Y):
                        yield h, x, c, l, y


INNER, OUTER = (2, 3, 4, 5), (7, 6, 1, 0)


def place(h, h2, x2):
    l = (INNER if h2 == h else OUTER)[x2]
    return l if h == 0 else L - 1 - l


def chunk(h, l):
    return next((h2, x2) for h2 in range(H) for x2 in range(X) if place(h, h2, x2) == l)


def weight_perm(k, d):
    return [
        (flat(h, x, c, l, y), flat(l // X, l % X, c ^ d, place(l // X, h ^ k, x), y))
        for h, x, c, l, y in coords()
    ]


def result_perm(k):
    return [
        (flat(h, x, c, l, y), flat(*chunk(h, l), c, L - 1 - x if h ^ k else x, y))
        for h, x, c, l, y in coords()
    ]


def shift(n, k):
    return [(i, (i + k) % n) for i in range(n)]


def contract_kernel(first_ref, second_ref, where_ref, w_ref, near_ref, far_ref, out_ref, acc_ref, s_ref):
    slots, rows, cols = w_ref.shape[1], w_ref.shape[2], w_ref.shape[3]

    @pl.when(pl.program_id(0) == 0)
    def _():
        acc_ref[...] = jnp.zeros_like(acc_ref)

        def add(slot, _):
            first, second = first_ref[slot], second_ref[slot]
            at_col = pl.multiple_of(first * cols, cols)
            for z in range(Y):
                half, part = z // 2, z % 2
                at_row = pl.multiple_of((half * OCC + second) * (2 * rows) + part * rows, rows)
                here = (pl.ds(at_row, rows), pl.ds(at_col, cols))
                acc_ref[here] += w_ref[z, slot].astype(jnp.float32)
            return 0

        lax.fori_loop(0, slots, add, 0)
        s_ref[...] = acc_ref[...].astype(jnp.bfloat16)

    depth = near_ref.shape[1]
    at_near = pl.multiple_of(where_ref[0] * depth, depth)
    at_far = pl.multiple_of((1 - where_ref[0]) * depth, depth)
    f32 = jnp.float32
    total = jnp.dot(near_ref[...], s_ref[pl.ds(at_near, depth)], preferred_element_type=f32)
    total += jnp.dot(far_ref[...], s_ref[pl.ds(at_far, depth)], preferred_element_type=f32)
    out_ref[...] = total.astype(jnp.bfloat16)


def contract(first, second, where, w, near, far):
    q, depth = near.shape
    cols = w.shape[3]
    block = q // L

    def of_step(s, *_):
        to = s // 2
        return jnp.where(s % 2 == 0, to, L - 1 - to), 0

    return pl.pallas_call(
        contract_kernel,
        grid_spec=pltpu.PrefetchScalarGridSpec(
            num_scalar_prefetch=3,
            grid=(L,),
            in_specs=[
                pl.BlockSpec(w.shape, lambda s, *_: (0, 0, 0, 0)),
                pl.BlockSpec((block, depth), of_step),
                pl.BlockSpec((block, depth), of_step),
            ],
            out_specs=pl.BlockSpec((block, OCC * cols), lambda s, *_: (s, 0)),
            scratch_shapes=[
                pltpu.VMEM((2 * depth, OCC * cols), jnp.float32),
                pltpu.VMEM((2 * depth, OCC * cols), jnp.bfloat16),
            ],
        ),
        out_shape=jax.ShapeDtypeStruct((q, OCC * cols), jnp.bfloat16),
        compiler_params=pltpu.CompilerParams(vmem_limit_bytes=32 * 1024 * 1024),
        cost_estimate=pl.CostEstimate(
            flops=2 * q * 2 * depth * OCC * cols, bytes_accessed=6 * 2**20, transcendentals=0
        ),
    )(first, second, where, w, near, far)


def on_device(amplitudes, fitting, coefficients, pair_list):
    h, c, y = lax.axis_index("h"), lax.axis_index("c"), lax.axis_index("y")
    f32, bf16 = jnp.float32, jnp.bfloat16

    def swap_core(v):
        return lax.ppermute(v, "c", shift(C, 1))

    def gather(v, axes, n):
        v = jnp.broadcast_to(v[None], (n,) + v.shape)
        return lax.all_to_all(v, axes, split_axis=0, concat_axis=0, tiled=True)

    q_own, occ, b_own = fitting.shape
    b_near = lax.all_gather(fitting, "l", axis=0, tiled=True)

    n_mu, n_a = coefficients.shape
    part = n_mu // Y
    c_other = swap_core(coefficients)
    mirror = [(i, H * L - 1 - i) for i in range(H * L)]
    piece = lax.dynamic_slice_in_dim(coefficients, y * part, part, 0)
    piece = lax.ppermute(piece, ("h", "l"), mirror)

    rows = amplitudes.shape[2]
    info = jnp.pad(pair_list.astype(bf16), ((0, rows - 1), (0, 126)))
    t_own = jnp.concatenate([amplitudes[0].T, info], axis=1)
    c_other, t_own = lax.optimization_barrier((c_other, t_own))
    t_all = gather(t_own, "x", X)
    t_all, piece = lax.optimization_barrier((t_all, piece))
    info = t_all[:, 0, n_a:]
    info = jnp.pad(info, ((0, 16 - X), (0, 0)))
    t_all = t_all.reshape(X * rows, -1)[:, :n_a]
    c_far = gather(piece, ("c", "y"), C * Y).reshape(C * n_mu, n_a)

    def weights(m):
        return lax.dot_general(
            t_all, m, (((1,), (1,)), ((), ())), preferred_element_type=f32
        ).astype(bf16)

    near = [weights(coefficients), weights(c_other)]
    far = weights(c_far)
    far = [lax.dynamic_slice_in_dim(far, (c ^ d) * n_mu, n_mu, 1) for d in range(C)]
    w = [
        lax.ppermute(jnp.concatenate([v, info], axis=0), AXES, weight_perm(k, d))
        for k, pieces in enumerate((near, far))
        for d, v in enumerate(pieces)
    ]
    w = jnp.stack(w)
    slots, n_b = H * C * X, X * rows
    pairs = w[:, n_b : n_b + X, :2].reshape(slots, 2).astype(jnp.int32)
    w = w[:, :n_b].reshape(slots, rows, n_mu)

    w, b_near = lax.optimization_barrier((w, b_near))
    w_all = gather(w, "y", Y)
    w_all = w_all.reshape(Y, slots, rows, n_mu)
    b_near = b_near.reshape(-1, occ * b_own)
    b_far = swap_core(b_near)

    where = c.astype(jnp.int32)[None]
    partial = contract(pairs[:, 0], pairs[:, 1], where, w_all, b_near, b_far)
    cols = partial.shape[1]
    partial = partial.reshape(X, 2 * q_own, cols)
    partial = lax.all_to_all(partial, "x", split_axis=0, concat_axis=0, tiled=True)
    summed = jnp.sum(partial.astype(f32), axis=0).astype(bf16)

    total = jnp.zeros((q_own, cols), f32)
    for k in range(H):
        piece = lax.dynamic_slice_in_dim(summed, (h ^ k) * q_own, q_own, 0)
        total += lax.ppermute(piece, AXES, result_perm(k)).astype(f32)
    return total.astype(bf16).reshape(q_own, occ, n_mu)


def solution(mesh):
    fine = Mesh(mesh.devices.reshape(H, X, C, L, Y), AXES)
    pair, aux = ("h", "x", "c"), ("l", "y")
    in_specs = (P(pair, None, aux), P(aux, None, pair), P(pair, None), P(pair, None))
    out_specs = P(aux, None, pair)
    return jax.shard_map(
        on_device, mesh=fine, in_specs=in_specs, out_specs=out_specs, check_vma=False
    )
```

```python
import jax
import jax.numpy as jnp
from jax import lax
from jax.experimental import pallas as pl
from jax.experimental.pallas import tpu as pltpu
from jax.sharding import Mesh, PartitionSpec as P

H, X, C, L, Y = 2, 4, 2, 8, 4
AXES = ("h", "x", "c", "l", "y")
OCC = 4


RING = [0, 2, 4, 6, 7, 5, 3, 1]


def flat(h, x, c, l, y):
    return (((h * X + x) * C + c) * L + l) * Y + y


def coords():
    for h in range(H):
        for x in range(X):
            for c in range(C):
                for l in range(L):
                    for y in range(Y):
                        yield h, x, c, l, y


INNER, OUTER = (2, 3, 4, 5), (7, 6, 1, 0)


def place(h, h2, x2):
    l = (INNER if h2 == h else OUTER)[x2]
    return l if h == 0 else L - 1 - l


def chunk(h, l):
    return next((h2, x2) for h2 in range(H) for x2 in range(X) if place(h, h2, x2) == l)


def weight_perm(k, d):
    return [
        (flat(h, x, c, l, y), flat(l // X, l % X, c ^ d, place(l // X, h ^ k, x), y))
        for h, x, c, l, y in coords()
    ]


def result_perm(k):
    return [
        (flat(h, x, c, l, y), flat(*chunk(h, l), c, L - 1 - x if h ^ k else x, y))
        for h, x, c, l, y in coords()
    ]


def shift(n, k):
    return [(i, (i + k) % n) for i in range(n)]


def contract_kernel(first_ref, second_ref, where_ref, w_ref, near_ref, far_ref, out_ref, acc_ref, s_ref):
    slots, rows, cols = w_ref.shape[1], w_ref.shape[2], w_ref.shape[3]

    @pl.when(pl.program_id(0) == 0)
    def _():
        acc_ref[...] = jnp.zeros_like(acc_ref)

        def add(slot, _):
            first, second = first_ref[slot], second_ref[slot]
            at_col = pl.multiple_of(first * cols, cols)
            for z in range(Y):
                half, part = z // 2, z % 2
                at_row = pl.multiple_of((half * OCC + second) * (2 * rows) + part * rows, rows)
                here = (pl.ds(at_row, rows), pl.ds(at_col, cols))
                acc_ref[here] += w_ref[z, slot].astype(jnp.float32)
            return 0

        lax.fori_loop(0, slots, add, 0)
        s_ref[...] = acc_ref[...].astype(jnp.bfloat16)

    depth = near_ref.shape[1]
    at_near = pl.multiple_of(where_ref[0] * depth, depth)
    at_far = pl.multiple_of((1 - where_ref[0]) * depth, depth)
    f32 = jnp.float32
    total = jnp.dot(near_ref[...], s_ref[pl.ds(at_near, depth)], preferred_element_type=f32)
    total += jnp.dot(far_ref[...], s_ref[pl.ds(at_far, depth)], preferred_element_type=f32)
    out_ref[...] = total.astype(jnp.bfloat16)


def contract(first, second, where, w, near, far):
    q, depth = near.shape
    cols = w.shape[3]
    block = q // L

    def of_step(s, *_):
        l = jnp.where(s % 2 == 0, s // 2, L - 1 - s // 2)
        return jnp.where(l % 2 == 0, l // 2, (2 * L - 1 - l) // 2), 0

    return pl.pallas_call(
        contract_kernel,
        grid_spec=pltpu.PrefetchScalarGridSpec(
            num_scalar_prefetch=3,
            grid=(L,),
            in_specs=[
                pl.BlockSpec(w.shape, lambda s, *_: (0, 0, 0, 0)),
                pl.BlockSpec((block, depth), of_step),
                pl.BlockSpec((block, depth), of_step),
            ],
            out_specs=pl.BlockSpec((block, OCC * cols), lambda s, *_: (s, 0)),
            scratch_shapes=[
                pltpu.VMEM((2 * depth, OCC * cols), jnp.float32),
                pltpu.VMEM((2 * depth, OCC * cols), jnp.bfloat16),
            ],
        ),
        out_shape=jax.ShapeDtypeStruct((q, OCC * cols), jnp.bfloat16),
        compiler_params=pltpu.CompilerParams(vmem_limit_bytes=32 * 1024 * 1024),
        cost_estimate=pl.CostEstimate(
            flops=2 * q * 2 * depth * OCC * cols, bytes_accessed=6 * 2**20, transcendentals=0
        ),
    )(first, second, where, w, near, far)


def on_device(amplitudes, fitting, coefficients, pair_list):
    h, c, y = lax.axis_index("h"), lax.axis_index("c"), lax.axis_index("y")
    f32, bf16 = jnp.float32, jnp.bfloat16

    def swap_core(v):
        return lax.ppermute(v, "c", shift(C, 1))

    def gather(v, axes, n):
        v = jnp.broadcast_to(v[None], (n,) + v.shape)
        return lax.all_to_all(v, axes, split_axis=0, concat_axis=0, tiled=True)

    q_own, occ, b_own = fitting.shape
    b_near = lax.all_gather(fitting, "l", axis=0, tiled=True, axis_index_groups=[RING])

    n_mu, n_a = coefficients.shape
    part = n_mu // Y
    c_other = swap_core(coefficients)
    mirror = [(i, H * L - 1 - i) for i in range(H * L)]
    piece = lax.dynamic_slice_in_dim(coefficients, y * part, part, 0)
    piece = lax.ppermute(piece, ("h", "l"), mirror)

    rows = amplitudes.shape[2]
    info = jnp.pad(pair_list.astype(bf16), ((0, rows - 1), (0, 126)))
    t_own = jnp.concatenate([amplitudes[0].T, info], axis=1)
    c_other, t_own = lax.optimization_barrier((c_other, t_own))
    t_all = gather(t_own, "x", X)
    t_all, piece = lax.optimization_barrier((t_all, piece))
    info = t_all[:, 0, n_a:]
    info = jnp.pad(info, ((0, 16 - X), (0, 0)))
    t_all = t_all.reshape(X * rows, -1)[:, :n_a]
    c_far = gather(piece, ("c", "y"), C * Y).reshape(C * n_mu, n_a)

    def weights(m):
        return lax.dot_general(
            t_all, m, (((1,), (1,)), ((), ())), preferred_element_type=f32
        ).astype(bf16)

    near = [weights(coefficients), weights(c_other)]
    far = weights(c_far)
    far = [lax.dynamic_slice_in_dim(far, (c ^ d) * n_mu, n_mu, 1) for d in range(C)]
    w = [
        lax.ppermute(jnp.concatenate([v, info], axis=0), AXES, weight_perm(k, d))
        for k, pieces in enumerate((near, far))
        for d, v in enumerate(pieces)
    ]
    w = jnp.stack(w)
    slots, n_b = H * C * X, X * rows
    pairs = w[:, n_b : n_b + X, :2].reshape(slots, 2).astype(jnp.int32)
    w = w[:, :n_b].reshape(slots, rows, n_mu)

    w, b_near = lax.optimization_barrier((w, b_near))
    w_all = gather(w, "y", Y)
    w_all = w_all.reshape(Y, slots, rows, n_mu)
    b_near = b_near.reshape(-1, occ * b_own)
    b_far = swap_core(b_near)

    where = c.astype(jnp.int32)[None]
    partial = contract(pairs[:, 0], pairs[:, 1], where, w_all, b_near, b_far)
    cols = partial.shape[1]
    partial = partial.reshape(X, 2 * q_own, cols)
    partial = lax.all_to_all(partial, "x", split_axis=0, concat_axis=0, tiled=True)
    summed = jnp.sum(partial.astype(f32), axis=0).astype(bf16)

    total = jnp.zeros((q_own, cols), f32)
    for k in range(H):
        piece = lax.dynamic_slice_in_dim(summed, (h ^ k) * q_own, q_own, 0)
        total += lax.ppermute(piece, AXES, result_perm(k)).astype(f32)
    return total.astype(bf16).reshape(q_own, occ, n_mu)


def solution(mesh):
    fine = Mesh(mesh.devices.reshape(H, X, C, L, Y), AXES)
    pair, aux = ("h", "x", "c"), ("l", "y")
    in_specs = (P(pair, None, aux), P(aux, None, pair), P(pair, None), P(pair, None))
    out_specs = P(aux, None, pair)
    return jax.shard_map(
        on_device, mesh=fine, in_specs=in_specs, out_specs=out_specs, check_vma=False
    )
```

```python
import jax
import jax.numpy as jnp
from jax import lax
from jax.experimental import pallas as pl
from jax.experimental.pallas import tpu as pltpu
from jax.sharding import Mesh, PartitionSpec as P

H, X, C, L, Y = 2, 4, 2, 8, 4
AXES = ("h", "x", "c", "l", "y")
OCC = 4


RING = [0, 2, 4, 6, 7, 5, 3, 1]


def flat(h, x, c, l, y):
    return (((h * X + x) * C + c) * L + l) * Y + y


def coords():
    for h in range(H):
        for x in range(X):
            for c in range(C):
                for l in range(L):
                    for y in range(Y):
                        yield h, x, c, l, y


INNER, OUTER = (2, 3, 4, 5), (7, 6, 1, 0)


def place(h, h2, x2):
    l = (INNER if h2 == h else OUTER)[x2]
    return l if h == 0 else L - 1 - l


def chunk(h, l):
    return next((h2, x2) for h2 in range(H) for x2 in range(X) if place(h, h2, x2) == l)


def weight_perm(k, d):
    return [
        (flat(h, x, c, l, y), flat(l // X, l % X, c ^ d, place(l // X, h ^ k, x), y))
        for h, x, c, l, y in coords()
    ]


def result_perm(k):
    return [
        (flat(h, x, c, l, y), flat(*chunk(h, l), c, L - 1 - x if h ^ k else x, y))
        for h, x, c, l, y in coords()
    ]


def shift(n, k):
    return [(i, (i + k) % n) for i in range(n)]


def contract_kernel(
    first_ref, second_ref, where_ref, w_ref, near_ref, near2_ref, far_ref, far2_ref, out_ref,
    acc_ref, s_ref
):
    slots, rows, cols = w_ref.shape[1:]

    @pl.when(pl.program_id(0) == 0)
    def _():
        acc_ref[...] = jnp.zeros_like(acc_ref)

        def add(slot, _):
            first, second = first_ref[slot], second_ref[slot]
            at_col = pl.multiple_of(first * cols, cols)
            for z in range(Y):
                half, part = z // 2, z % 2
                at_row = pl.multiple_of((half * OCC + second) * (2 * rows) + part * rows, rows)
                here = (pl.ds(at_row, rows), pl.ds(at_col, cols))
                acc_ref[here] += w_ref[z, slot].astype(jnp.float32)
            return 0

        lax.fori_loop(0, slots, add, 0)
        s_ref[...] = acc_ref[...].astype(jnp.bfloat16)

    block, depth = near_ref.shape
    at_near = pl.multiple_of(where_ref[0] * depth, depth)
    at_far = pl.multiple_of((1 - where_ref[0]) * depth, depth)
    f32 = jnp.float32
    for part, (near, far) in enumerate(((near_ref, far_ref), (near2_ref, far2_ref))):
        total = jnp.dot(near[...], s_ref[pl.ds(at_near, depth)], preferred_element_type=f32)
        total += jnp.dot(far[...], s_ref[pl.ds(at_far, depth)], preferred_element_type=f32)
        out_ref[part * block : (part + 1) * block] = total.astype(jnp.bfloat16)


def contract(first, second, where, w, near, far):
    q, depth = near.shape
    cols = w.shape[3]
    block = q // L

    def rows_of(part):
        def of_step(x, *_):
            l = L - 1 - x if part else x
            return jnp.where(l % 2 == 0, l // 2, (2 * L - 1 - l) // 2), 0

        return pl.BlockSpec((block, depth), of_step)

    return pl.pallas_call(
        contract_kernel,
        grid_spec=pltpu.PrefetchScalarGridSpec(
            num_scalar_prefetch=3,
            grid=(X,),
            in_specs=[pl.BlockSpec(w.shape, lambda s, *_: (0, 0, 0, 0))]
            + [rows_of(0), rows_of(1)] * 2,
            out_specs=pl.BlockSpec((2 * block, OCC * cols), lambda s, *_: (s, 0)),
            scratch_shapes=[
                pltpu.VMEM((2 * depth, OCC * cols), jnp.float32),
                pltpu.VMEM((2 * depth, OCC * cols), jnp.bfloat16),
            ],
        ),
        out_shape=jax.ShapeDtypeStruct((q, OCC * cols), jnp.bfloat16),
        compiler_params=pltpu.CompilerParams(vmem_limit_bytes=32 * 1024 * 1024),
        cost_estimate=pl.CostEstimate(
            flops=2 * q * 2 * depth * OCC * cols, bytes_accessed=6 * 2**20, transcendentals=0
        ),
    )(first, second, where, w, near, near, far, far)


def on_device(amplitudes, fitting, coefficients, pair_list):
    h, c, y = lax.axis_index("h"), lax.axis_index("c"), lax.axis_index("y")
    f32, bf16 = jnp.float32, jnp.bfloat16

    def swap_core(v):
        return lax.ppermute(v, "c", shift(C, 1))

    def gather(v, axes, n):
        v = jnp.broadcast_to(v[None], (n,) + v.shape)
        return lax.all_to_all(v, axes, split_axis=0, concat_axis=0, tiled=True)

    q_own, occ, b_own = fitting.shape
    b_near = fitting.reshape(q_own, occ * b_own)
    b_near = lax.all_gather(b_near, "l", axis=0, tiled=True, axis_index_groups=[RING])

    n_mu, n_a = coefficients.shape
    part = n_mu // Y
    c_other = swap_core(coefficients)
    mirror = [(i, H * L - 1 - i) for i in range(H * L)]
    piece = lax.dynamic_slice_in_dim(coefficients, y * part, part, 0)
    piece = lax.ppermute(piece, ("h", "l"), mirror)

    rows = amplitudes.shape[2]
    info = jnp.pad(pair_list.astype(bf16), ((0, rows - 1), (0, 126)))
    t_own = jnp.concatenate([amplitudes[0].T, info], axis=1)
    t_all = gather(t_own, "x", X)
    info = t_all[:, 0, n_a:]
    info = jnp.pad(info, ((0, 16 - X), (0, 0)))
    t_all = t_all.reshape(X * rows, -1)[:, :n_a]
    c_far = jnp.zeros((n_mu, n_a), bf16)
    for k in range(Y):
        v = lax.ppermute(piece, "y", shift(Y, k)) if k else piece
        c_far = lax.dynamic_update_slice_in_dim(c_far, v, (y - k) % Y * part, 0)

    def weights(m):
        return lax.dot_general(
            t_all, m, (((1,), (1,)), ((), ())), preferred_element_type=f32
        ).astype(bf16)

    near = [weights(coefficients), weights(c_other)]
    far = [weights(c_far), weights(swap_core(c_far))]
    w = [
        lax.ppermute(jnp.concatenate([v, info], axis=0), AXES, weight_perm(k, d))
        for k, pieces in enumerate((near, far))
        for d, v in enumerate(pieces)
    ]
    w = jnp.stack(w)
    slots, n_b = H * C * X, X * rows
    pairs = w[:, n_b : n_b + X, :2].reshape(slots, 2).astype(jnp.int32)
    w = w[:, :n_b].reshape(slots, rows, n_mu)

    w, b_near = lax.optimization_barrier((w, b_near))
    b_far = swap_core(b_near)

    w_all = gather(w, "y", Y)
    w_all = w_all.reshape(Y, slots, rows, n_mu)

    where = c.astype(jnp.int32)[None]
    partial = contract(pairs[:, 0], pairs[:, 1], where, w_all, b_near, b_far)
    cols = partial.shape[1]
    partial = partial.reshape(X, 2 * q_own, cols)
    partial = lax.all_to_all(partial, "x", split_axis=0, concat_axis=0, tiled=True)
    summed = jnp.sum(partial.astype(f32), axis=0).astype(bf16)

    total = jnp.zeros((q_own, cols), f32)
    for k in range(H):
        piece = lax.dynamic_slice_in_dim(summed, (h ^ k) * q_own, q_own, 0)
        total += lax.ppermute(piece, AXES, result_perm(k)).astype(f32)
    return total.astype(bf16).reshape(q_own, occ, n_mu)


def solution(mesh):
    fine = Mesh(mesh.devices.reshape(H, X, C, L, Y), AXES)
    pair, aux = ("h", "x", "c"), ("l", "y")
    in_specs = (P(pair, None, aux), P(aux, None, pair), P(pair, None), P(pair, None))
    out_specs = P(aux, None, pair)
    return jax.shard_map(
        on_device, mesh=fine, in_specs=in_specs, out_specs=out_specs, check_vma=False
    )
```

```python
import jax
import jax.numpy as jnp
from jax import lax
from jax.experimental import pallas as pl
from jax.experimental.pallas import tpu as pltpu
from jax.sharding import Mesh, PartitionSpec as P

H, X, C, L, Y = 2, 4, 2, 8, 4
AXES = ("h", "x", "c", "l", "y")
OCC = 4


RING = [0, 2, 4, 6, 7, 5, 3, 1]


def flat(h, x, c, l, y):
    return (((h * X + x) * C + c) * L + l) * Y + y


def coords():
    for h in range(H):
        for x in range(X):
            for c in range(C):
                for l in range(L):
                    for y in range(Y):
                        yield h, x, c, l, y


PLACE = ((6, 7, 3, 2, 1, 0, 4, 5), (7, 6, 2, 3, 0, 1, 4, 5))
ROWS = ((2, 6), (3, 7), (4, 0), (5, 1))


def place(h, h2, x2):
    return PLACE[h][h2 * X + x2]


def chunk(h, l):
    return divmod(PLACE[h].index(l), X)


def weight_perm(k, d):
    return [
        (flat(h, x, c, l, y), flat(l // X, l % X, c ^ d, place(l // X, h ^ k, x), y))
        for h, x, c, l, y in coords()
    ]


def result_perm(k):
    return [
        (flat(h, x, c, l, y), flat(*chunk(h, l), c, ROWS[x][h ^ k], y))
        for h, x, c, l, y in coords()
    ]


def shift(n, k):
    return [(i, (i + k) % n) for i in range(n)]


def contract_kernel(
    where_ref, first_ref, second_ref, w_ref, near_ref, far_ref, out_ref, acc_ref, s_ref
):
    slots, rows, cols = w_ref.shape[1:]

    @pl.when(pl.program_id(0) == 0)
    def _():
        acc_ref[...] = jnp.zeros_like(acc_ref)

        def add(slot, _):
            first, second = first_ref[slot], second_ref[slot]
            at_col = pl.multiple_of(first * cols, cols)
            for z in range(Y):
                half, part = z // 2, z % 2
                at_row = pl.multiple_of((half * OCC + second) * (2 * rows) + part * rows, rows)
                here = (pl.ds(at_row, rows), pl.ds(at_col, cols))
                acc_ref[here] += w_ref[z, slot].astype(jnp.float32)
            return 0

        lax.fori_loop(0, slots, add, 0)
        s_ref[...] = acc_ref[...].astype(jnp.bfloat16)

    depth = near_ref.shape[1]
    at_near = pl.multiple_of(where_ref[0] * depth, depth)
    at_far = pl.multiple_of((1 - where_ref[0]) * depth, depth)
    f32 = jnp.float32
    total = jnp.dot(near_ref[...], s_ref[pl.ds(at_near, depth)], preferred_element_type=f32)
    total += jnp.dot(far_ref[...], s_ref[pl.ds(at_far, depth)], preferred_element_type=f32)
    out_ref[...] = total.astype(jnp.bfloat16)


def contract(where, first, second, w, near, far):
    q, depth = near.shape
    cols = OCC * w.shape[3]
    block = q // L
    rows = [pl.BlockSpec((block, depth), lambda x, where, *_: (where[1 + x], 0))] * 2
    return pl.pallas_call(
        contract_kernel,
        grid_spec=pltpu.PrefetchScalarGridSpec(
            num_scalar_prefetch=3,
            grid=(X,),
            in_specs=[pl.BlockSpec(w.shape, lambda x, *_: (0, 0, 0, 0))] + rows,
            out_specs=pl.BlockSpec((block, cols), lambda x, *_: (x, 0)),
            scratch_shapes=[
                pltpu.VMEM((2 * depth, cols), jnp.float32),
                pltpu.VMEM((2 * depth, cols), jnp.bfloat16),
            ],
        ),
        out_shape=jax.ShapeDtypeStruct((X * block, cols), jnp.bfloat16),
        compiler_params=pltpu.CompilerParams(vmem_limit_bytes=32 * 1024 * 1024),
        cost_estimate=pl.CostEstimate(
            flops=2 * q * depth * cols, bytes_accessed=4 * 2**20, transcendentals=0
        ),
    )(where, first, second, w, near, far)


def on_device(amplitudes, fitting, coefficients, pair_list):
    h, c, y = lax.axis_index("h"), lax.axis_index("c"), lax.axis_index("y")
    f32, bf16 = jnp.float32, jnp.bfloat16

    def swap_core(v):
        return lax.ppermute(v, "c", shift(C, 1))

    def gather(v, axes, n):
        v = jnp.broadcast_to(v[None], (n,) + v.shape)
        return lax.all_to_all(v, axes, split_axis=0, concat_axis=0, tiled=True)

    q_own, occ, b_own = fitting.shape
    b_near = fitting.reshape(q_own, occ * b_own)
    b_near = lax.all_gather(b_near, "l", axis=0, tiled=True, axis_index_groups=[RING])

    n_mu, n_a = coefficients.shape
    part = n_mu // Y
    c_other = swap_core(coefficients)
    mirror = [(i, H * L - 1 - i) for i in range(H * L)]
    piece = lax.dynamic_slice_in_dim(coefficients, y * part, part, 0)
    piece = lax.ppermute(piece, ("h", "l"), mirror)

    rows = amplitudes.shape[2]
    info = jnp.pad(pair_list.astype(bf16), ((0, rows - 1), (0, 126)))
    t_own = jnp.concatenate([amplitudes[0].T, info], axis=1)
    t_all = gather(t_own, "x", X)
    info = t_all[:, 0, n_a:]
    info = jnp.pad(info, ((0, 16 - X), (0, 0)))
    t_all = t_all.reshape(X * rows, -1)[:, :n_a]
    c_far = jnp.zeros((n_mu, n_a), bf16)
    for k in range(Y):
        v = lax.ppermute(piece, "y", shift(Y, k)) if k else piece
        c_far = lax.dynamic_update_slice_in_dim(c_far, v, (y - k) % Y * part, 0)

    def weights(m):
        return lax.dot_general(
            t_all, m, (((1,), (1,)), ((), ())), preferred_element_type=f32
        ).astype(bf16)

    near = [weights(coefficients), weights(c_other)]
    far = [weights(c_far), weights(swap_core(c_far))]
    w = [
        lax.ppermute(jnp.concatenate([v, info], axis=0), AXES, weight_perm(k, d))
        for k, pieces in enumerate((near, far))
        for d, v in enumerate(pieces)
    ]
    w = jnp.stack(w)
    slots, n_b = H * C * X, X * rows
    pairs = w[:, n_b : n_b + X, :2].reshape(slots, 2).astype(jnp.int32)
    w = w[:, :n_b].reshape(slots, rows, n_mu)

    w, b_near = lax.optimization_barrier((w, b_near))
    b_far = swap_core(b_near)

    w_all = gather(w, "y", Y)
    w_all = w_all.reshape(Y, slots, rows, n_mu)

    at = jnp.asarray([[RING.index(two[s]) for two in ROWS] for s in range(H)], jnp.int32)
    total = 0
    for k in range(H):
        where = jnp.where(h == k, at[0], at[1])
        where = jnp.concatenate([c.astype(jnp.int32)[None], where])
        v = contract(where, pairs[:, 0], pairs[:, 1], w_all, b_near, b_far)
        v = v.reshape(X, q_own, -1)
        v = lax.all_to_all(v, "x", split_axis=0, concat_axis=0, tiled=True)
        v = jnp.sum(v.astype(f32), axis=0).astype(bf16)
        total += lax.ppermute(v, AXES, result_perm(k)).astype(f32)
    return total.astype(bf16).reshape(q_own, occ, n_mu)


def solution(mesh):
    fine = Mesh(mesh.devices.reshape(H, X, C, L, Y), AXES)
    pair, aux = ("h", "x", "c"), ("l", "y")
    in_specs = (P(pair, None, aux), P(aux, None, pair), P(pair, None), P(pair, None))
    out_specs = P(aux, None, pair)
    return jax.shard_map(
        on_device, mesh=fine, in_specs=in_specs, out_specs=out_specs, check_vma=False
    )
```

```python
import jax
import jax.numpy as jnp
from jax import lax
from jax.experimental import pallas as pl
from jax.experimental.pallas import tpu as pltpu
from jax.sharding import Mesh, PartitionSpec as P

H, X, C, L, Y = 2, 4, 2, 8, 4
AXES = ("h", "x", "c", "l", "y")
OCC = 4


RING = [0, 2, 4, 6, 7, 5, 3, 1]


def flat(h, x, c, l, y):
    return (((h * X + x) * C + c) * L + l) * Y + y


def coords():
    for h in range(H):
        for x in range(X):
            for c in range(C):
                for l in range(L):
                    for y in range(Y):
                        yield h, x, c, l, y


INNER, OUTER = (2, 3, 4, 5), (7, 6, 1, 0)


def place(h, h2, x2):
    l = (INNER if h2 == h else OUTER)[x2]
    return l if h == 0 else L - 1 - l


def chunk(h, l):
    return next((h2, x2) for h2 in range(H) for x2 in range(X) if place(h, h2, x2) == l)


def weight_perm(k):
    return [
        (flat(h, x, c, l, y), flat(l // X, l % X, c, place(l // X, h ^ k, x), y))
        for h, x, c, l, y in coords()
    ]


def result_perm(k):
    return [
        (flat(h, x, c, l, y), flat(*chunk(h, l), c, L - 1 - x if h ^ k else x, y))
        for h, x, c, l, y in coords()
    ]


def shift(n, k):
    return [(i, (i + k) % n) for i in range(n)]


def contract_kernel(where_ref, first_ref, second_ref, w_ref, near_ref, far_ref, out_ref, s_ref):
    slots, rows, cols = w_ref.shape[1:]

    @pl.when(pl.program_id(0) == 0)
    def _():
        s_ref[...] = jnp.zeros_like(s_ref)
        for slot in range(slots):
            at_row = second_ref[slot] * (2 * rows)
            at_col = pl.ds(pl.multiple_of(first_ref[slot] * cols, cols), cols)
            for z in range(Y):
                row = (z // 2) * OCC * 2 * rows + at_row + (z % 2) * rows
                here = (pl.ds(pl.multiple_of(row, rows), rows), at_col)
                s_ref[here] += w_ref[z, slot]

    depth = near_ref.shape[1]
    at_near = pl.multiple_of(where_ref[0] * depth, depth)
    at_far = pl.multiple_of((1 - where_ref[0]) * depth, depth)
    f32 = jnp.float32
    total = jnp.dot(near_ref[...], s_ref[pl.ds(at_near, depth)], preferred_element_type=f32)
    total += jnp.dot(far_ref[...], s_ref[pl.ds(at_far, depth)], preferred_element_type=f32)
    out_ref[...] = total.astype(jnp.bfloat16)


def contract(where, first, second, w, near, far):
    q, depth = near.shape
    cols = OCC * w.shape[3]
    block = q // L
    rows = [pl.BlockSpec((block, depth), lambda x, where, *_: (where[1 + x], 0))] * 2
    return pl.pallas_call(
        contract_kernel,
        grid_spec=pltpu.PrefetchScalarGridSpec(
            num_scalar_prefetch=3,
            grid=(X,),
            in_specs=[pl.BlockSpec(w.shape, lambda x, *_: (0, 0, 0, 0))] + rows,
            out_specs=pl.BlockSpec((block, cols), lambda x, *_: (x, 0)),
            scratch_shapes=[pltpu.VMEM((2 * depth, cols), jnp.bfloat16)],
        ),
        out_shape=jax.ShapeDtypeStruct((X * block, cols), jnp.bfloat16),
        compiler_params=pltpu.CompilerParams(vmem_limit_bytes=32 * 1024 * 1024),
        cost_estimate=pl.CostEstimate(
            flops=2 * q * depth * cols, bytes_accessed=4 * 2**20, transcendentals=0
        ),
    )(where, first, second, w, near, far)


def on_device(amplitudes, fitting, coefficients, pair_list):
    h, c, y = lax.axis_index("h"), lax.axis_index("c"), lax.axis_index("y")
    f32, bf16 = jnp.float32, jnp.bfloat16

    def swap_core(v):
        return lax.ppermute(v, "c", shift(C, 1))

    def gather(v, axes, n):
        v = jnp.broadcast_to(v[None], (n,) + v.shape)
        return lax.all_to_all(v, axes, split_axis=0, concat_axis=0, tiled=True)

    q_own, occ, b_own = fitting.shape
    b_near = fitting.reshape(q_own, occ * b_own)
    b_near = lax.all_gather(b_near, "l", axis=0, tiled=True, axis_index_groups=[RING])

    n_mu, n_a = coefficients.shape
    part = n_mu // Y
    mirror = [(i, H * L - 1 - i) for i in range(H * L)]
    piece = lax.dynamic_slice_in_dim(coefficients, y * part, part, 0)
    piece = lax.ppermute(piece, ("h", "l"), mirror)

    rows = amplitudes.shape[2]
    info = jnp.pad(pair_list.astype(bf16), ((0, rows - 1), (0, 126)))
    t_own = jnp.concatenate([amplitudes[0].T, info], axis=1)
    t_all = gather(t_own, "x", X)
    t_all, piece = lax.optimization_barrier((t_all, piece))
    halves = (t_all, swap_core(t_all))
    slots, n_b = C * X, C * X * rows
    info = [v[:, 0, n_a:] for v in halves] + [jnp.zeros((16 - slots, n_mu), bf16)]
    halves = [v.reshape(X * rows, -1)[:, :n_a] for v in halves]

    c_far = jnp.zeros((n_mu, n_a), bf16)
    for k in range(Y):
        v = lax.ppermute(piece, "y", shift(Y, k)) if k else piece
        c_far = lax.dynamic_update_slice_in_dim(c_far, v, (y - k) % Y * part, 0)

    w = []
    for k, m in enumerate((coefficients, c_far)):
        v = [
            lax.dot_general(t, m, (((1,), (1,)), ((), ())), preferred_element_type=f32)
            for t in halves
        ]
        v = jnp.concatenate([t.astype(bf16) for t in v] + info, axis=0)
        w.append(lax.ppermute(v, AXES, weight_perm(k)))
    w = jnp.stack(w)
    slots *= H
    pairs = w[:, n_b : n_b + C * X, :2].reshape(slots, 2).astype(jnp.int32)
    w = w[:, :n_b].reshape(slots, rows, n_mu)

    w, b_near = lax.optimization_barrier((w, b_near))
    b_far = swap_core(b_near)

    w_all = gather(w, "y", Y)
    w_all = w_all.reshape(Y, slots, rows, n_mu)

    at = [[RING.index(x) for x in range(X)], [RING.index(L - 1 - x) for x in range(X)]]
    at = jnp.asarray(at, jnp.int32)
    total = 0
    for k in range(H):
        where = jnp.where(h == k, at[0], at[1])
        where = jnp.concatenate([c.astype(jnp.int32)[None], where])
        v = contract(where, pairs[:, 0], pairs[:, 1], w_all, b_near, b_far)
        v = v.reshape(X, q_own, -1)
        v = lax.all_to_all(v, "x", split_axis=0, concat_axis=0, tiled=True)
        v = jnp.sum(v.astype(f32), axis=0).astype(bf16)
        total += lax.ppermute(v, AXES, result_perm(k)).astype(f32)
    return total.astype(bf16).reshape(q_own, occ, n_mu)


def solution(mesh):
    fine = Mesh(mesh.devices.reshape(H, X, C, L, Y), AXES)
    pair, aux = ("h", "x", "c"), ("l", "y")
    in_specs = (P(pair, None, aux), P(aux, None, pair), P(pair, None), P(pair, None))
    out_specs = P(aux, None, pair)
    return jax.shard_map(
        on_device, mesh=fine, in_specs=in_specs, out_specs=out_specs, check_vma=False
    )
```

```python
import jax
import jax.numpy as jnp
from jax import lax
from jax.experimental import pallas as pl
from jax.experimental.pallas import tpu as pltpu
from jax.sharding import Mesh, PartitionSpec as P

H, X, C, L, Y = 2, 4, 2, 8, 4
AXES = ("h", "x", "c", "l", "y")
OCC = 4


RING = [0, 2, 4, 6, 7, 5, 3, 1]


def flat(h, x, c, l, y):
    return (((h * X + x) * C + c) * L + l) * Y + y


def coords():
    for h in range(H):
        for x in range(X):
            for c in range(C):
                for l in range(L):
                    for y in range(Y):
                        yield h, x, c, l, y


INNER, OUTER = (2, 3, 4, 5), (7, 6, 1, 0)


def place(h, h2, x2):
    l = (INNER if h2 == h else OUTER)[x2]
    return l if h == 0 else L - 1 - l


def chunk(h, l):
    return next((h2, x2) for h2 in range(H) for x2 in range(X) if place(h, h2, x2) == l)


def weight_perm(k, d):
    return [
        (flat(h, x, c, l, y), flat(l // X, l % X, c ^ d, place(l // X, h ^ k, x), y))
        for h, x, c, l, y in coords()
    ]


def result_perm(k):
    return [
        (flat(h, x, c, l, y), flat(*chunk(h, l), c, L - 1 - x if h ^ k else x, y))
        for h, x, c, l, y in coords()
    ]


def shift(n, k):
    return [(i, (i + k) % n) for i in range(n)]


def contract_kernel(where_ref, first_ref, second_ref, w_ref, near_ref, far_ref, out_ref, s_ref):
    slots, rows, cols = w_ref.shape[1:]

    @pl.when(pl.program_id(0) == 0)
    def _():
        s_ref[...] = jnp.zeros_like(s_ref)
        for slot in range(slots):
            at_row = second_ref[slot] * (2 * rows)
            at_col = pl.ds(pl.multiple_of(first_ref[slot] * cols, cols), cols)
            for z in range(Y):
                row = (z // 2) * OCC * 2 * rows + at_row + (z % 2) * rows
                here = (pl.ds(pl.multiple_of(row, rows), rows), at_col)
                s_ref[here] += w_ref[z, slot]

    depth = near_ref.shape[1]
    at_near = pl.multiple_of(where_ref[0] * depth, depth)
    at_far = pl.multiple_of((1 - where_ref[0]) * depth, depth)
    f32 = jnp.float32
    total = jnp.dot(near_ref[...], s_ref[pl.ds(at_near, depth)], preferred_element_type=f32)
    total += jnp.dot(far_ref[...], s_ref[pl.ds(at_far, depth)], preferred_element_type=f32)
    out_ref[...] = total.astype(jnp.bfloat16)


def contract(where, first, second, w, near, far):
    q, depth = near.shape
    cols = OCC * w.shape[3]
    block = q // L
    rows = [pl.BlockSpec((block, depth), lambda x, where, *_: (where[1 + x], 0))] * 2
    return pl.pallas_call(
        contract_kernel,
        grid_spec=pltpu.PrefetchScalarGridSpec(
            num_scalar_prefetch=3,
            grid=(X,),
            in_specs=[pl.BlockSpec(w.shape, lambda x, *_: (0, 0, 0, 0))] + rows,
            out_specs=pl.BlockSpec((block, cols), lambda x, *_: (x, 0)),
            scratch_shapes=[pltpu.VMEM((2 * depth, cols), jnp.bfloat16)],
        ),
        out_shape=jax.ShapeDtypeStruct((X * block, cols), jnp.bfloat16),
        compiler_params=pltpu.CompilerParams(vmem_limit_bytes=32 * 1024 * 1024),
        cost_estimate=pl.CostEstimate(
            flops=2 * q * depth * cols, bytes_accessed=4 * 2**20, transcendentals=0
        ),
    )(where, first, second, w, near, far)


def on_device(amplitudes, fitting, coefficients, pair_list):
    h, c, y = lax.axis_index("h"), lax.axis_index("c"), lax.axis_index("y")
    f32, bf16 = jnp.float32, jnp.bfloat16

    def swap_core(v):
        return lax.ppermute(v, "c", shift(C, 1))

    def gather(v, axes, n):
        v = jnp.broadcast_to(v[None], (n,) + v.shape)
        return lax.all_to_all(v, axes, split_axis=0, concat_axis=0, tiled=True)

    q_own, occ, b_own = fitting.shape
    b_near = fitting.reshape(q_own, occ * b_own)
    b_near = lax.all_gather(b_near, "l", axis=0, tiled=True, axis_index_groups=[RING])

    n_mu, n_a = coefficients.shape
    part = n_mu // Y
    c_other = swap_core(coefficients)
    mirror = [(i, H * L - 1 - i) for i in range(H * L)]
    piece = lax.dynamic_slice_in_dim(coefficients, y * part, part, 0)
    piece = lax.ppermute(piece, ("h", "l"), mirror)

    rows = amplitudes.shape[2]
    info = jnp.pad(pair_list.astype(bf16), ((0, rows - 1), (0, 126)))
    t_own = jnp.concatenate([amplitudes[0].T, info], axis=1)
    t_all = gather(t_own, "x", X)
    info = t_all[:, 0, n_a:]
    info = jnp.pad(info, ((0, 16 - X), (0, 0)))
    t_all = t_all.reshape(X * rows, -1)[:, :n_a]
    c_far = jnp.zeros((n_mu, n_a), bf16)
    for k in range(Y):
        v = lax.ppermute(piece, "y", shift(Y, k)) if k else piece
        c_far = lax.dynamic_update_slice_in_dim(c_far, v, (y - k) % Y * part, 0)

    def weights(m):
        return lax.dot_general(
            t_all, m, (((1,), (1,)), ((), ())), preferred_element_type=f32
        ).astype(bf16)

    near = [weights(coefficients), weights(c_other)]
    far = [weights(c_far), weights(swap_core(c_far))]
    w = [
        lax.ppermute(jnp.concatenate([v, info], axis=0), AXES, weight_perm(k, d))
        for k, pieces in enumerate((near, far))
        for d, v in enumerate(pieces)
    ]
    w = jnp.stack(w)
    slots, n_b = H * C * X, X * rows
    pairs = w[:, n_b : n_b + X, :2].reshape(slots, 2).astype(jnp.int32)
    w = w[:, :n_b].reshape(slots, rows, n_mu)

    w, b_near = lax.optimization_barrier((w, b_near))
    b_far = swap_core(b_near)

    w_all = gather(w, "y", Y)
    w_all = w_all.reshape(Y, slots, rows, n_mu)

    at = [[RING.index(x) for x in range(X)], [RING.index(L - 1 - x) for x in range(X)]]
    at = jnp.asarray(at, jnp.int32)
    total = 0
    for k in range(H):
        where = jnp.where(h == k, at[0], at[1])
        where = jnp.concatenate([c.astype(jnp.int32)[None], where])
        v = contract(where, pairs[:, 0], pairs[:, 1], w_all, b_near, b_far)
        v = v.reshape(X, q_own, -1)
        v = lax.all_to_all(v, "x", split_axis=0, concat_axis=0, tiled=True)
        v = jnp.sum(v.astype(f32), axis=0).astype(bf16)
        total += lax.ppermute(v, AXES, result_perm(k)).astype(f32)
    return total.astype(bf16).reshape(q_own, occ, n_mu)


def solution(mesh):
    fine = Mesh(mesh.devices.reshape(H, X, C, L, Y), AXES)
    pair, aux = ("h", "x", "c"), ("l", "y")
    in_specs = (P(pair, None, aux), P(aux, None, pair), P(pair, None), P(pair, None))
    out_specs = P(aux, None, pair)
    return jax.shard_map(
        on_device, mesh=fine, in_specs=in_specs, out_specs=out_specs, check_vma=False
    )
```

```python
import jax
import jax.numpy as jnp
from jax import lax
from jax.experimental import pallas as pl
from jax.experimental.pallas import tpu as pltpu
from jax.sharding import Mesh, PartitionSpec as P

H, X, C, L, Y = 2, 4, 2, 8, 4
AXES = ("h", "x", "c", "l", "y")
OCC = 4


RING = [0, 2, 4, 6, 7, 5, 3, 1]


def flat(h, x, c, l, y):
    return (((h * X + x) * C + c) * L + l) * Y + y


def coords():
    for h in range(H):
        for x in range(X):
            for c in range(C):
                for l in range(L):
                    for y in range(Y):
                        yield h, x, c, l, y


INNER, OUTER = (2, 3, 4, 5), (0, 1, 6, 7)


def place(h, h2, x2):
    return (INNER if h2 == h else OUTER)[x2]


def chunk(h, l):
    return next((h2, x2) for h2 in range(H) for x2 in range(X) if place(h, h2, x2) == l)


def weight_perm(k, d):
    return [
        (flat(h, x, c, l, y), flat(l // X, l % X, c ^ d, place(l // X, h ^ k, x), y))
        for h, x, c, l, y in coords()
    ]


def result_perm(k):
    return [
        (flat(h, x, c, l, y), flat(*chunk(h, l), c, L - 1 - x if h ^ k else x, y))
        for h, x, c, l, y in coords()
    ]


def shift(n, k):
    return [(i, (i + k) % n) for i in range(n)]


def contract_kernel(where_ref, first_ref, second_ref, w_ref, near_ref, far_ref, out_ref, s_ref):
    slots, rows, cols = w_ref.shape[1:]

    @pl.when(pl.program_id(0) == 0)
    def _():
        s_ref[...] = jnp.zeros_like(s_ref)
        for slot in range(slots):
            at_row = second_ref[slot] * (2 * rows)
            at_col = pl.ds(pl.multiple_of(first_ref[slot] * cols, cols), cols)
            for z in range(Y):
                row = (z // 2) * OCC * 2 * rows + at_row + (z % 2) * rows
                here = (pl.ds(pl.multiple_of(row, rows), rows), at_col)
                s_ref[here] += w_ref[z, slot]

    depth = near_ref.shape[1]
    at_near = pl.multiple_of(where_ref[0] * depth, depth)
    at_far = pl.multiple_of((1 - where_ref[0]) * depth, depth)
    f32 = jnp.float32
    total = jnp.dot(near_ref[...], s_ref[pl.ds(at_near, depth)], preferred_element_type=f32)
    total += jnp.dot(far_ref[...], s_ref[pl.ds(at_far, depth)], preferred_element_type=f32)
    out_ref[...] = total.astype(jnp.bfloat16)


def contract(where, first, second, w, near, far):
    q, depth = near.shape
    cols = OCC * w.shape[3]
    block = q // L
    rows = [pl.BlockSpec((block, depth), lambda x, where, *_: (where[1 + x], 0))] * 2
    return pl.pallas_call(
        contract_kernel,
        grid_spec=pltpu.PrefetchScalarGridSpec(
            num_scalar_prefetch=3,
            grid=(X,),
            in_specs=[pl.BlockSpec(w.shape, lambda x, *_: (0, 0, 0, 0))] + rows,
            out_specs=pl.BlockSpec((block, cols), lambda x, *_: (x, 0)),
            scratch_shapes=[pltpu.VMEM((2 * depth, cols), jnp.bfloat16)],
        ),
        out_shape=jax.ShapeDtypeStruct((X * block, cols), jnp.bfloat16),
        compiler_params=pltpu.CompilerParams(vmem_limit_bytes=32 * 1024 * 1024),
        cost_estimate=pl.CostEstimate(
            flops=2 * q * depth * cols, bytes_accessed=4 * 2**20, transcendentals=0
        ),
    )(where, first, second, w, near, far)


def on_device(amplitudes, fitting, coefficients, pair_list):
    h, c, y = lax.axis_index("h"), lax.axis_index("c"), lax.axis_index("y")
    f32, bf16 = jnp.float32, jnp.bfloat16

    def swap_core(v):
        return lax.ppermute(v, "c", shift(C, 1))

    def gather(v, axes, n):
        v = jnp.broadcast_to(v[None], (n,) + v.shape)
        return lax.all_to_all(v, axes, split_axis=0, concat_axis=0, tiled=True)

    q_own, occ, b_own = fitting.shape
    b_near = fitting.reshape(q_own, occ * b_own)
    b_near = lax.all_gather(b_near, "l", axis=0, tiled=True, axis_index_groups=[RING])

    n_mu, n_a = coefficients.shape
    part = n_mu // Y
    c_other = swap_core(coefficients)
    mirror = [(i, H * L - 1 - i) for i in range(H * L)]
    piece = lax.dynamic_slice_in_dim(coefficients, y * part, part, 0)
    piece = lax.ppermute(piece, ("h", "l"), mirror)

    rows = amplitudes.shape[2]
    info = jnp.pad(pair_list.astype(bf16), ((0, rows - 1), (0, 126)))
    t_own = jnp.concatenate([amplitudes[0].T, info], axis=1)
    t_all = gather(t_own, "x", X)
    info = t_all[:, 0, n_a:]
    info = jnp.pad(info, ((0, 16 - X), (0, 0)))
    t_all = t_all.reshape(X * rows, -1)[:, :n_a]
    c_far = jnp.zeros((n_mu, n_a), bf16)
    for k in range(Y):
        v = lax.ppermute(piece, "y", shift(Y, k)) if k else piece
        c_far = lax.dynamic_update_slice_in_dim(c_far, v, (y - k) % Y * part, 0)

    def weights(m):
        return lax.dot_general(
            t_all, m, (((1,), (1,)), ((), ())), preferred_element_type=f32
        ).astype(bf16)

    near = [weights(coefficients), weights(c_other)]
    far = [weights(c_far), weights(swap_core(c_far))]
    w = [
        lax.ppermute(jnp.concatenate([v, info], axis=0), AXES, weight_perm(k, d))
        for k, pieces in enumerate((near, far))
        for d, v in enumerate(pieces)
    ]
    w = jnp.stack(w)
    slots, n_b = H * C * X, X * rows
    pairs = w[:, n_b : n_b + X, :2].reshape(slots, 2).astype(jnp.int32)
    w = w[:, :n_b].reshape(slots, rows, n_mu)

    w, b_near = lax.optimization_barrier((w, b_near))
    b_far = swap_core(b_near)

    w_all = gather(w, "y", Y)
    w_all = w_all.reshape(Y, slots, rows, n_mu)

    at = [[RING.index(x) for x in range(X)], [RING.index(L - 1 - x) for x in range(X)]]
    at = jnp.asarray(at, jnp.int32)
    total = 0
    for k in range(H):
        where = jnp.where(h == k, at[0], at[1])
        where = jnp.concatenate([c.astype(jnp.int32)[None], where])
        v = contract(where, pairs[:, 0], pairs[:, 1], w_all, b_near, b_far)
        v = v.reshape(X, q_own, -1)
        v = lax.all_to_all(v, "x", split_axis=0, concat_axis=0, tiled=True)
        v = jnp.sum(v.astype(f32), axis=0).astype(bf16)
        total += lax.ppermute(v, AXES, result_perm(k)).astype(f32)
    return total.astype(bf16).reshape(q_own, occ, n_mu)


def solution(mesh):
    fine = Mesh(mesh.devices.reshape(H, X, C, L, Y), AXES)
    pair, aux = ("h", "x", "c"), ("l", "y")
    in_specs = (P(pair, None, aux), P(aux, None, pair), P(pair, None), P(pair, None))
    out_specs = P(aux, None, pair)
    return jax.shard_map(
        on_device, mesh=fine, in_specs=in_specs, out_specs=out_specs, check_vma=False
    )
```

```python
import jax
import jax.numpy as jnp
from jax import lax
from jax.experimental import pallas as pl
from jax.experimental.pallas import tpu as pltpu
from jax.sharding import Mesh, PartitionSpec as P

H, X, C, L, Y = 2, 4, 2, 8, 4
AXES = ("h", "x", "c", "l", "y")
OCC = 4


RING = [0, 2, 4, 6, 7, 5, 3, 1]


def flat(h, x, c, l, y):
    return (((h * X + x) * C + c) * L + l) * Y + y


def coords():
    for h in range(H):
        for x in range(X):
            for c in range(C):
                for l in range(L):
                    for y in range(Y):
                        yield h, x, c, l, y


INNER, OUTER = (2, 3, 4, 5), (7, 6, 1, 0)


def place(h, h2, x2):
    l = (INNER if h2 == h else OUTER)[x2]
    return l if h == 0 else L - 1 - l


def chunk(h, l):
    return next((h2, x2) for h2 in range(H) for x2 in range(X) if place(h, h2, x2) == l)


def weight_perm(k, d):
    return [
        (flat(h, x, c, l, y), flat(l // X, l % X, c ^ d, place(l // X, h ^ k, x), y))
        for h, x, c, l, y in coords()
    ]


def result_perm(k):
    return [
        (flat(h, x, c, l, y), flat(*chunk(h, l), c, L - 1 - x if h ^ k else x, y))
        for h, x, c, l, y in coords()
    ]


def shift(n, k):
    return [(i, (i + k) % n) for i in range(n)]


def contract_kernel(where_ref, first_ref, second_ref, w_ref, near_ref, far_ref, out_ref, s_ref):
    slots, rows, cols = w_ref.shape[1:]

    @pl.when(pl.program_id(0) == 0)
    def _():
        s_ref[...] = jnp.zeros_like(s_ref)
        for slot in range(slots):
            at_row = second_ref[slot] * (2 * rows)
            at_col = pl.ds(pl.multiple_of(first_ref[slot] * cols, cols), cols)
            for z in range(Y):
                row = (z // 2) * OCC * 2 * rows + at_row + (z % 2) * rows
                here = (pl.ds(pl.multiple_of(row, rows), rows), at_col)
                s_ref[here] += w_ref[z, slot]

    depth = near_ref.shape[1]
    at_near = pl.multiple_of(where_ref[0] * depth, depth)
    at_far = pl.multiple_of((1 - where_ref[0]) * depth, depth)
    f32 = jnp.float32
    total = jnp.dot(near_ref[...], s_ref[pl.ds(at_near, depth)], preferred_element_type=f32)
    total += jnp.dot(far_ref[...], s_ref[pl.ds(at_far, depth)], preferred_element_type=f32)
    out_ref[...] = total.astype(jnp.bfloat16)


def contract(where, first, second, w, near, far):
    q, depth = near.shape
    cols = OCC * w.shape[3]
    block = q // L
    rows = [pl.BlockSpec((block, depth), lambda x, where, *_: (where[1 + x], 0))] * 2
    return pl.pallas_call(
        contract_kernel,
        grid_spec=pltpu.PrefetchScalarGridSpec(
            num_scalar_prefetch=3,
            grid=(X,),
            in_specs=[pl.BlockSpec(w.shape, lambda x, *_: (0, 0, 0, 0))] + rows,
            out_specs=pl.BlockSpec((block, cols), lambda x, *_: (x, 0)),
            scratch_shapes=[pltpu.VMEM((2 * depth, cols), jnp.bfloat16)],
        ),
        out_shape=jax.ShapeDtypeStruct((X * block, cols), jnp.bfloat16),
        compiler_params=pltpu.CompilerParams(vmem_limit_bytes=32 * 1024 * 1024),
        cost_estimate=pl.CostEstimate(
            flops=2 * q * depth * cols, bytes_accessed=4 * 2**20, transcendentals=0
        ),
    )(where, first, second, w, near, far)


def on_device(amplitudes, fitting, coefficients, pair_list):
    h, c, y = lax.axis_index("h"), lax.axis_index("c"), lax.axis_index("y")
    f32, bf16 = jnp.float32, jnp.bfloat16

    def swap_core(v):
        return lax.ppermute(v, "c", shift(C, 1))

    def gather(v, axes, n):
        v = jnp.broadcast_to(v[None], (n,) + v.shape)
        return lax.all_to_all(v, axes, split_axis=0, concat_axis=0, tiled=True)

    q_own, occ, b_own = fitting.shape
    b_near = fitting.reshape(q_own, occ * b_own)
    b_near = lax.all_gather(b_near, "l", axis=0, tiled=True, axis_index_groups=[RING])

    n_mu, n_a = coefficients.shape
    part = n_mu // Y
    c_other = swap_core(coefficients)
    mirror = [(i, H * L - 1 - i) for i in range(H * L)]
    piece = lax.dynamic_slice_in_dim(coefficients, y * part, part, 0)
    piece = lax.ppermute(piece, ("h", "l"), mirror)

    rows = amplitudes.shape[2]
    info = jnp.pad(pair_list.astype(bf16), ((0, rows - 1), (0, 126)))
    t_own = jnp.concatenate([amplitudes[0].T, info], axis=1)
    t_all = gather(t_own, "x", X)
    info = t_all[:, 0, n_a:]
    info = jnp.pad(info, ((0, 16 - X), (0, 0)))
    t_all = t_all.reshape(X * rows, -1)[:, :n_a]
    c_far = jnp.zeros((n_mu, n_a), bf16)
    for k in range(Y):
        v = lax.ppermute(piece, "y", shift(Y, k)) if k else piece
        c_far = lax.dynamic_update_slice_in_dim(c_far, v, (y - k) % Y * part, 0)

    def weights(m):
        return lax.dot_general(
            t_all, m, (((1,), (1,)), ((), ())), preferred_element_type=f32
        ).astype(bf16)

    near = [weights(coefficients), weights(c_other)]
    far = [weights(c_far), weights(swap_core(c_far))]
    w = []
    for k, pieces in enumerate((near, far)):
        v = jnp.stack([jnp.concatenate([v, info], axis=0) for v in pieces])
        v = lax.ppermute(v, AXES, weight_perm(k, 0))
        w += [v[0], swap_core(v[1])]
    w = jnp.stack(w)
    slots, n_b = H * C * X, X * rows
    pairs = w[:, n_b : n_b + X, :2].reshape(slots, 2).astype(jnp.int32)
    w = w[:, :n_b].reshape(slots, rows, n_mu)

    w, b_near = lax.optimization_barrier((w, b_near))
    b_far = swap_core(b_near)

    w_all = gather(w, "y", Y)
    w_all = w_all.reshape(Y, slots, rows, n_mu)

    at = [[RING.index(x) for x in range(X)], [RING.index(L - 1 - x) for x in range(X)]]
    at = jnp.asarray(at, jnp.int32)
    total = 0
    for k in range(H):
        where = jnp.where(h == k, at[0], at[1])
        where = jnp.concatenate([c.astype(jnp.int32)[None], where])
        v = contract(where, pairs[:, 0], pairs[:, 1], w_all, b_near, b_far)
        v = v.reshape(X, q_own, -1)
        v = lax.all_to_all(v, "x", split_axis=0, concat_axis=0, tiled=True)
        v = jnp.sum(v.astype(f32), axis=0).astype(bf16)
        total += lax.ppermute(v, AXES, result_perm(k)).astype(f32)
    return total.astype(bf16).reshape(q_own, occ, n_mu)


def solution(mesh):
    fine = Mesh(mesh.devices.reshape(H, X, C, L, Y), AXES)
    pair, aux = ("h", "x", "c"), ("l", "y")
    in_specs = (P(pair, None, aux), P(aux, None, pair), P(pair, None), P(pair, None))
    out_specs = P(aux, None, pair)
    return jax.shard_map(
        on_device, mesh=fine, in_specs=in_specs, out_specs=out_specs, check_vma=False
    )
```
